256 devices in a mesh: pair: 8 (over y, x_lo), zone: 32 (over x_hi, z, core).
Axes of the slice: x: 4 (x_hi: 2, x_lo: 2; x = x_hi * 2 + x_lo), y: 4, z: 8, core: 2. Of those that a mesh axis runs over, the one named last changes fastest.
Arguments:
- vel_a: bfloat16 [64, 2, 3, 57344], P('pair', None, None, 'zone'), may hold values from -4.1875 to 4.1875
- vel_b: bfloat16 [256, 2, 3, 57344], P('pair', None, None, 'zone'), may hold values from -4.1875 to 4.1875
- panel_modes: bfloat16 [200, 57344], P(None, 'zone'), may hold values from -0.0234375 to 0.0234375
- modal_stress: bfloat16 [200, 16384], P(None, 'zone'), may hold values from -0.4375 to 0.4375
- freq_a: float32 [64], P('pair'), may hold values from 0.3 to 1.5
- freq_b: float32 [256], replicated, may hold values from 0.3 to 1.5
- mode_freq: float32 [200], replicated, may hold values from 0.6 to 3
- damping: float32 [200], replicated, may hold values from 0.05 to 0.2
Outputs:
- stress: bfloat16 [16384, 2, 64, 256], P('zone', None, 'pair')
The draws below stay inside these ranges and needn't reach their ends.
All inputs are finite; a program needn't handle non-finite values.
Results may differ from the reference program's by a relative error of at most 0.0058.
Values may be sent and summed in bfloat16 or wider, within the bound.
A program may use at most 64 MiB of HBM per device.

```python
import math
import jax
import jax.numpy as jnp
from jax import lax

MODES = 200
NB = 256
NA = 64
PANELS = 57344
ELEMENTS = 16384


def level_of(own_key, shape, cuts, smallest, top_value):
    gain = 1.0
    for position, shards_of in cuts:
        steps = jax.random.uniform(jax.random.fold_in(jax.random.fold_in(own_key, 6), position), (shards_of,), jnp.float32, smallest / len(cuts), top_value / len(cuts))
        gain = gain * jnp.repeat(jnp.exp(steps), shape[position] // shards_of).reshape((-1,) + (1,) * (len(shape) - 1 - position))
    return gain


def normal_values(own_key, shape, scale, most, pieces=(), dtype=jnp.bfloat16):
    entries = scale * jax.random.normal(own_key, shape, jnp.float32)
    if pieces:
        entries = entries * level_of(own_key, shape, pieces, -0.22, 0.18)
    return jnp.clip(entries, -most, most).astype(dtype)


def setup_inputs(seed: int = 0) -> dict:
    key_list = jax.random.split(jax.random.key(seed), 9)
    vel_a = normal_values(key_list[0], (NA, 2, 3, PANELS), 0.7, 4.1875, ((0, 8), (3, 32)))
    vel_b = normal_values(key_list[1], (NB, 2, 3, PANELS), 0.7, 4.1875, ((0, 8), (3, 32)))
    panel_modes = normal_values(key_list[2], (MODES, PANELS), PANELS ** -0.5, 0.0234375, ((1, 32),))
    modal_stress = normal_values(key_list[3], (MODES, ELEMENTS), MODES ** -0.5, 0.4375, ((1, 32),))
    freq_a = jnp.clip(0.3 + 1.2 * jax.random.uniform(key_list[4], (NA,), jnp.float32) ** level_of(key_list[4], (NA,), ((0, 8),), -0.2, 0.2), 0.3, 1.5)
    freq_b = jnp.clip(jax.random.uniform(key_list[5], (NB,), jnp.float32, 0.3, 1.5), 0.3, 1.5)
    mode_freq = jnp.clip(jnp.exp(jax.random.uniform(key_list[6], (MODES,), jnp.float32, math.log(0.6), math.log(3.0))), 0.6, 3.0)
    damping = jnp.clip(jnp.exp(jax.random.uniform(key_list[7], (MODES,), jnp.float32, math.log(0.05), math.log(0.2))), 0.05, 0.2)
    return dict(vel_a=vel_a, vel_b=vel_b, panel_modes=panel_modes, modal_stress=modal_stress, freq_a=freq_a, freq_b=freq_b, mode_freq=mode_freq, damping=damping)


def quadratic(first_vel, second_vel):
    pressure_re = jnp.zeros((first_vel.shape[0], second_vel.shape[0], first_vel.shape[3]), jnp.float32)
    pressure_im = jnp.zeros((first_vel.shape[0], second_vel.shape[0], first_vel.shape[3]), jnp.float32)
    for component in range(3):
        first_re = first_vel[:, None, 0, component]
        first_im = first_vel[:, None, 1, component]
        second_re = second_vel[None, :, 0, component]
        second_im = second_vel[None, :, 1, component]
        pressure_re = pressure_re + first_re * second_re - first_im * second_im
        pressure_im = pressure_im + first_re * second_im + first_im * second_re
    return jnp.stack([-0.5 * pressure_re, -0.5 * pressure_im]).astype(jnp.bfloat16)


def respond(first_freq, second_freq, forces, mode_freq, damping):
    sum_freq = first_freq[:, None] + second_freq[None, :]
    mode_square = (mode_freq * mode_freq)[:, None, None]
    detuning = mode_square - sum_freq[None] * sum_freq[None]
    damping_term = (2.0 * damping * mode_freq)[:, None, None] * sum_freq[None]
    denominator = detuning * detuning + damping_term * damping_term
    recept_re = mode_square * detuning / denominator
    recept_im = -mode_square * damping_term / denominator
    response_re = recept_re * forces[:, 0] - recept_im * forces[:, 1]
    response_im = recept_re * forces[:, 1] + recept_im * forces[:, 0]
    return jnp.stack([response_re, response_im], axis=1).astype(jnp.bfloat16)


def reference(vel_a, vel_b, panel_modes, modal_stress, freq_a, freq_b, mode_freq, damping):
    second_vel = vel_b.astype(jnp.float32)
    modes_count = panel_modes.shape[0]
    second_count = vel_b.shape[0]

    def per_first(items):
        first_one, first_freq = items
        pressure = quadratic(first_one[None].astype(jnp.float32), second_vel)
        flat = pressure.reshape(2 * second_count, pressure.shape[3])
        forces = jnp.dot(panel_modes, flat.T, preferred_element_type=jnp.float32)
        forces = forces.reshape(modes_count, 2, 1, second_count)
        response = respond(first_freq[None], freq_b, forces, mode_freq, damping)
        result = jnp.dot(modal_stress.T, response.reshape(modes_count, 2 * second_count), preferred_element_type=jnp.float32)
        return result.reshape(modal_stress.shape[1], 2, second_count).astype(jnp.bfloat16)

    stacked = lax.map(per_first, (vel_a, freq_a))
    return jnp.transpose(stacked, (1, 2, 0, 3))
```

```python
import functools

import jax
import jax.numpy as jnp
from jax import lax
from jax.experimental import pallas as pl
from jax.experimental.pallas import tpu as pltpu
from jax.sharding import PartitionSpec as P

MESH = pl.DeviceIdType.MESH
F32 = jnp.float32
BF16 = jnp.bfloat16

A8 = 8
B32 = 32
KD = 1792
KT = KD // 128
M = 200
MH = 104
STEPS = ("plus", "minus")


def main_kernel(
    va, vb, modes, fa, fbt, msq, mdf,
    r_out,
    vel, fas, vf, uf, prs, grid_f, tx_sib, rx_sib, tx_z, rx_z, tx_x, rx_x, resp,
    vel_ss, vel_rs, fa_ss, fa_rs, sib_ss, sib_rs, z_ss, z_rs, x_ss, x_rs,
    a_ss, a_rs, g_ss, g_rs, gs_ss, gs_rs, loc_sem,
):
    pair = lax.axis_index("pair")
    zone = lax.axis_index("zone")
    y, xl = pair // 2, pair % 2
    core, z, xh = zone % 2, (zone // 2) % 8, zone // 16

    def dev(dy=0, dx=0, dz=0, dh=0, dc=0):
        return (
            ((y + dy) % 4) * 2 + (xl + dx) % 2,
            (((xh + dh) % 2) * 8 + (z + dz + 8) % 8) * 2 + (core + dc) % 2,
        )

    def exchange_peer(yq):
        return (yq * 2 + core, (xh * 8 + z) * 2 + xl)

    cross = xl != core

    barrier = pltpu.get_barrier_semaphore()
    pair_peers = [(dy, dx) for dy in range(4) for dx in range(2) if (dy, dx) != (0, 0)]
    for dy, dx in pair_peers:
        pl.semaphore_signal(barrier, inc=1, device_id=dev(dy=dy, dx=dx), device_id_type=MESH)
    for kw in (dict(dc=1), dict(dz=1), dict(dz=-1), dict(dh=1)):
        pl.semaphore_signal(barrier, inc=1, device_id=dev(**kw), device_id_type=MESH)

    @pl.when(cross)
    def _():
        for yq in range(4):
            pl.semaphore_signal(barrier, inc=1, device_id=exchange_peer(yq), device_id_type=MESH)

    pl.semaphore_wait(barrier, 11 + 4 * ((xl + core) % 2))

    def vel_copy(src, dst, k, to, half=None):
        s = vel.at[src] if half is None else vel.at[src, :, pl.ds(half, KD // 2)]
        d = vel.at[dst] if half is None else vel.at[dst, :, pl.ds(half, KD // 2)]
        return pltpu.make_async_remote_copy(
            src_ref=s, dst_ref=d, send_sem=vel_ss.at[k], recv_sem=vel_rs.at[k],
            device_id=to, device_id_type=MESH)

    own_vel = pltpu.make_async_copy(va, vel.at[0], loc_sem.at[0])
    own_vel.start()
    own_fa = pltpu.make_async_copy(fa, fas.at[0], loc_sem.at[1])
    own_fa.start()
    own_vel.wait()
    own_fa.wait()
    c_x = vel_copy(0, 1, 0, dev(dx=1))
    c_yp = vel_copy(0, 6, 1, dev(dy=1))
    c_ym = vel_copy(0, 2, 2, dev(dy=3))
    c_xyp = vel_copy(1, 7, 3, dev(dy=1))
    c_xym = vel_copy(1, 3, 4, dev(dy=3))
    c_fyp = vel_copy(6, 4, 5, dev(dy=1), 0)
    c_fym = vel_copy(2, 4, 6, dev(dy=3), KD // 2)
    c_x2 = vel_copy(4, 5, 7, dev(dx=1))
    c_x.start()
    c_yp.start()
    c_ym.start()
    fa_copies = []
    for n, (dy, dx) in enumerate(pair_peers):
        slot = 2 * ((4 - dy) % 4) + dx
        cp = pltpu.make_async_remote_copy(
            src_ref=fas.at[0], dst_ref=fas.at[slot], send_sem=fa_ss.at[n], recv_sem=fa_rs.at[n],
            device_id=dev(dy=dy, dx=dx), device_id_type=MESH)
        cp.start()
        fa_copies.append(cp)

    def zero_pad(n, _):
        grid_f[n // 4, 4 + n % 4, 96:104, :] = jnp.zeros((8, 128), F32)
        tx_sib[n // 4, 4 + n % 4, 96:104, :] = jnp.zeros((8, 128), BF16)
        return 0

    lax.fori_loop(0, 16, zero_pad, 0)

    def prep(kt, _):
        lanes = pl.ds(pl.multiple_of(kt * 128, 128), 128)
        for c in range(3):
            vr = vb[c * 64:c * 64 + 32, lanes].astype(F32)
            vi = vb[c * 64 + 32:c * 64 + 64, lanes].astype(F32)
            vf[kt, c * 3] = vr
            vf[kt, c * 3 + 1] = vi - vr
            vf[kt, c * 3 + 2] = vr + vi
        return 0

    lax.fori_loop(0, KT, prep, 0)

    def sib_copy(j):
        return pltpu.make_async_remote_copy(
            src_ref=tx_sib.at[j], dst_ref=rx_sib.at[j], send_sem=sib_ss.at[j], recv_sem=sib_rs.at[j],
            device_id=dev(dc=1), device_id_type=MESH)

    def block(i, _):
        j, dx = i // 2, i % 2
        dy = j + (j // 2) * (5 - 2 * j)
        slot = 2 * dy + dx

        @pl.when(i == 1)
        def _():
            c_x.wait_recv()
            c_xyp.start()
            c_xym.start()

        @pl.when(i == 2)
        def _():
            c_yp.wait_recv()
            c_fyp.start()
            c_ym.wait_recv()
            c_fym.start()

        @pl.when(i == 3)
        def _():
            c_xym.wait_recv()

        @pl.when(i == 5)
        def _():
            c_xyp.wait_recv()
            c_fyp.wait_recv()
            c_fym.wait_recv()
            c_x2.start()

        @pl.when(i == 7)
        def _():
            c_x2.wait_recv()

        def tile(kt, _):
            lanes = pl.ds(pl.multiple_of(kt * 128, 128), 128)
            for c in range(3):
                both = vel[slot, c * 16:c * 16 + 16, lanes].astype(F32)
                ur, ui = both[0:8] * -0.5, both[8:16] * -0.5
                uf[c * 24:c * 24 + 8] = ur
                uf[c * 24 + 8:c * 24 + 16] = ui
                uf[c * 24 + 16:c * 24 + 24] = ur + ui
            for a in range(A8):
                row = (a // 2) * 128 + (a % 2) * 32
                for half in range(2):
                    b = slice(half * 16, half * 16 + 16)
                    k1 = k2 = k3 = None
                    for c in range(3):
                        ur = uf[c * 24 + a:c * 24 + a + 1, :]
                        ui = uf[c * 24 + 8 + a:c * 24 + 8 + a + 1, :]
                        us = uf[c * 24 + 16 + a:c * 24 + 16 + a + 1, :]
                        t1 = vf[kt, c * 3, b, :] * us
                        t2 = vf[kt, c * 3 + 1, b, :] * ur
                        t3 = vf[kt, c * 3 + 2, b, :] * ui
                        k1 = t1 if k1 is None else k1 + t1
                        k2 = t2 if k2 is None else k2 + t2
                        k3 = t3 if k3 is None else k3 + t3
                    prs[row + half * 16:row + half * 16 + 16, lanes] = (k1 - k3).astype(BF16)
                    prs[row + 64 + half * 16:row + 64 + half * 16 + 16, lanes] = (k1 + k2).astype(BF16)
            return 0

        lax.fori_loop(0, KT, tile, 0)
        mine = (xl + dx) % 2 == core

        for zl in range(4):
            f = lax.dot_general(
                modes[...], prs[zl * 128:zl * 128 + 128, :], (((1,), (1,)), ((), ())),
                preferred_element_type=F32)

            @pl.when(mine)
            def _():
                grid_f[j, zl] = f[0:104]
                grid_f[j, 4 + zl, 0:96] = f[104:200]

            @pl.when(jnp.logical_not(mine))
            def _():
                tx_sib[j, zl] = f[0:104].astype(BF16)
                tx_sib[j, 4 + zl, 0:96] = f[104:200].astype(BF16)

        @pl.when(jnp.logical_not(mine))
        def _():
            sib_copy(j).start()

        return 0

    lax.fori_loop(0, 8, block, 0)

    for cp in (c_x, c_yp, c_ym, c_xyp, c_xym, c_fyp, c_fym, c_x2):
        cp.wait_send()

    def add_sibling(j, _):
        sib_copy(j).wait_recv()

        def add(t, _):
            grid_f[j, t] = grid_f[j, t] + rx_sib[j, t].astype(F32)
            return 0

        lax.fori_loop(0, 8, add, 0)
        return 0

    lax.fori_loop(0, 4, add_sibling, 0)

    def z_copy(d, s, j):
        return pltpu.make_async_remote_copy(
            src_ref=tx_z.at[d, s, j], dst_ref=rx_z.at[d, s, j],
            send_sem=z_ss.at[d, s, j], recv_sem=z_rs.at[d, s, j],
            device_id=dev(dz=1 if d == 0 else -1), device_id_type=MESH)

    for s in range(4):
        for j in range(4):
            for d in range(2):
                first = 0 if j % 2 == d else 1
                if s < first:
                    continue
                t = (z + (4 - s) + 8) % 8 if d == 0 else (z - (4 - s) + 8) % 8
                value = grid_f[j, t]
                if s > first:
                    z_copy(d, s - 1, j).wait_recv()
                    value = value + rx_z[d, s - 1, j].astype(F32)
                tx_z[d, s, j] = value.astype(BF16)
                z_copy(d, s, j).start()

    def x_copy(j):
        return pltpu.make_async_remote_copy(
            src_ref=tx_x.at[j], dst_ref=rx_x.at[j], send_sem=x_ss.at[j], recv_sem=x_rs.at[j],
            device_id=dev(dh=1), device_id_type=MESH)

    for j in range(4):
        z_copy(0, 3, j).wait_recv()
        z_copy(1, 3, j).wait_recv()
        value = grid_f[j, z] + rx_z[0, 3, j].astype(F32) + rx_z[1, 3, j].astype(F32)
        grid_f[j, z] = value
        tx_x[j] = value.astype(BF16)
        x_copy(j).start()

    for cp in fa_copies:
        cp.wait()

    def a_copy(j):
        yq = (y + (0, 1, 3, 2)[j]) % 4
        return pltpu.make_async_remote_copy(
            src_ref=resp.at[j], dst_ref=r_out.at[z, xl, y],
            send_sem=a_ss.at[j], recv_sem=a_rs.at[y],
            device_id=exchange_peer(yq), device_id_type=MESH)

    lane = lax.broadcasted_iota(jnp.int32, (1, 128), 1)
    second = (lane // 32) % 2 == 1
    sign = jnp.where(lane < 64, -1.0, 1.0).astype(F32)
    zh, zl = z // 4, z % 4
    s2, g0 = msq[zh], mdf[zh]
    fb_row = fbt[pl.ds(pair, 1), :]
    for j in range(4):
        slot = 2 * (0, 1, 3, 2)[j] + (core + xl) % 2
        x_copy(j).wait_recv()
        f = grid_f[j, z] + rx_x[j].astype(F32)
        fa0 = fas[slot, pl.ds(zl * 2, 1), :]
        fa1 = fas[slot, pl.ds(zl * 2 + 1, 1), :]
        w = jnp.where(second, fa1, fa0) + fb_row
        t = s2 - w * w
        g = g0 * w
        inv = 1.0 / (t * t + g * g)
        re = s2 * t * inv
        im = -s2 * g * inv
        out = (re * f + im * (sign * pltpu.roll(f, 64, 1))).astype(BF16)
        if j == 0:
            @pl.when(cross)
            def _():
                resp[j] = out
                a_copy(j).start()

            @pl.when(jnp.logical_not(cross))
            def _():
                r_out[z, xl, y] = out
        else:
            resp[j] = out
            a_copy(j).start()

    def a_arrival(yq):
        return pltpu.make_async_remote_copy(
            src_ref=resp.at[0], dst_ref=r_out.at[z, core, yq],
            send_sem=a_ss.at[0], recv_sem=a_rs.at[yq],
            device_id=dev(dc=1), device_id_type=MESH)

    for dy in range(1, 4):
        a_arrival((y + dy) % 4).wait_recv()

    @pl.when(cross)
    def _():
        a_arrival(y).wait_recv()

    def g_copy(d, dist, h):
        src = (z - dist + 8) % 8 if d == 0 else (z + dist) % 8
        part = r_out.at[src, core, pl.ds(2 * h, 2)]
        return pltpu.make_async_remote_copy(
            src_ref=part, dst_ref=part, send_sem=g_ss.at[d, dist, h], recv_sem=g_rs.at[d, dist, h],
            device_id=dev(dz=1 if d == 0 else -1), device_id_type=MESH)

    def g_arrival(d, dist, h):
        src = (z - dist - 1 + 8) % 8 if d == 0 else (z + dist + 1) % 8
        part = r_out.at[src, core, pl.ds(2 * h, 2)]
        return pltpu.make_async_remote_copy(
            src_ref=part, dst_ref=part, send_sem=g_ss.at[d, dist, h], recv_sem=g_rs.at[d, dist, h],
            device_id=dev(dc=1), device_id_type=MESH)

    def sib_chunk(n, dz, h, mine=True):
        part = r_out.at[(z + dz + 8) % 8, core if mine else 1 - core, pl.ds(2 * h, 2)]
        return pltpu.make_async_remote_copy(
            src_ref=part, dst_ref=part, send_sem=gs_ss.at[n], recv_sem=gs_rs.at[n],
            device_id=dev(dc=1), device_id_type=MESH)

    chunks = []
    for dist in range(4):
        for h in range(2):
            for d in range(2):
                if dist > 0:
                    g_arrival(d, dist - 1, h).wait_recv()
                if dist < 3 or d == h:
                    g_copy(d, dist, h).start()
                if dist > 0 or d == 0:
                    dz = -dist if d == 0 else dist
                    sib_chunk(len(chunks), dz, h).start()
                    chunks.append((dz, h))
    for h in range(2):
        g_arrival(h, 3, h).wait_recv()
        sib_chunk(len(chunks), -4, h).start()
        chunks.append((-4, h))

    for n, (dz, h) in enumerate(chunks):
        sib_chunk(n, dz, h, mine=False).wait_recv()

    def drain(j, _):
        sib_copy(j).wait_send()
        x_copy(j).wait_send()
        return 0

    lax.fori_loop(0, 4, drain, 0)
    for s in range(4):
        for j in range(4):
            for d in range(2):
                if s >= (0 if j % 2 == d else 1):
                    z_copy(d, s, j).wait_send()
    for j in range(1, 4):
        a_copy(j).wait_send()

    @pl.when(cross)
    def _():
        a_copy(0).wait_send()

    for dist in range(4):
        for h in range(2):
            for d in range(2):
                if dist < 3 or d == h:
                    g_copy(d, dist, h).wait_send()
    for n, (dz, h) in enumerate(chunks):
        sib_chunk(n, dz, h).wait_send()


def stress_kernel(st, r_in, out, rhs, acc):
    @pl.when(pl.program_id(0) == 0)
    def _():
        lane = lax.broadcasted_iota(jnp.int32, (1, 128), 1) // 32

        def arrange(n, _):
            zh, zl, hp = n // 8, (n // 2) % 4, n % 2
            blocks = [r_in[zh * 4 + zl, i % 2, hp * 2 + i // 2].astype(F32) for i in range(4)]
            for g in range(4):
                row = None
                for i in range(4):
                    part = blocks[i] if i == g else pltpu.roll(blocks[i], ((i - g) * 32) % 128, 1)
                    row = part if row is None else jnp.where(lane == i, part, row)
                idx = (g // 2) * 8 + zl * 2 + g % 2
                rhs[idx, zh, :, pl.ds(pl.multiple_of(hp * 128, 128), 128)] = row.astype(BF16)
            return 0

        lax.fori_loop(0, 16, arrange, 0)

    for ra in range(16):
        r = rhs[ra].reshape(2 * MH, 256)
        acc[:, ra, :] = lax.dot_general(
            st[...], r, (((1,), (0,)), ((), ())), preferred_element_type=F32)
    out[...] = acc[...].reshape(out.shape).astype(BF16)


def local(vel_a, vel_b, panel_modes, modal_stress, freq_a, freq_b, mode_freq, damping):
    va = jnp.transpose(vel_a, (2, 1, 0, 3)).reshape(48, KD)
    vb = jnp.transpose(vel_b, (2, 1, 0, 3)).reshape(192, KD)
    fa = jnp.broadcast_to(freq_a[:, None], (A8, 128))
    fbt = jnp.tile(freq_b.reshape(8, B32), (1, 4))
    mf = jnp.pad(mode_freq, (0, 2 * MH - M), constant_values=1.0)
    dm = jnp.pad(damping, (0, 2 * MH - M), constant_values=0.1)
    msq = jnp.broadcast_to((mf * mf)[:, None], (2 * MH, 128)).reshape(2, MH, 128)
    mdf = jnp.broadcast_to((2.0 * dm * mf)[:, None], (2 * MH, 128)).reshape(2, MH, 128)
    vm = pl.BlockSpec(memory_space=pltpu.VMEM)
    dma = pltpu.SemaphoreType.DMA
    r = pl.pallas_call(
        main_kernel,
        out_shape=jax.ShapeDtypeStruct((8, 2, 4, MH, 128), BF16),
        in_specs=[vm] * 7,
        out_specs=vm,
        scratch_shapes=[
            pltpu.VMEM((8, 48, KD), BF16),
            pltpu.VMEM((8, A8, 128), F32),
            pltpu.VMEM((KT, 9, B32, 128), F32),
            pltpu.VMEM((72, 128), F32),
            pltpu.VMEM((512, KD), BF16),
            pltpu.VMEM((4, 8, MH, 128), F32),
            pltpu.VMEM((4, 8, MH, 128), BF16),
            pltpu.VMEM((4, 8, MH, 128), BF16),
            pltpu.VMEM((2, 4, 4, MH, 128), BF16),
            pltpu.VMEM((2, 4, 4, MH, 128), BF16),
            pltpu.VMEM((4, MH, 128), BF16),
            pltpu.VMEM((4, MH, 128), BF16),
            pltpu.VMEM((4, MH, 128), BF16),
            dma((8,)), dma((8,)), dma((7,)), dma((7,)), dma((4,)), dma((4,)),
            dma((2, 4, 4)), dma((2, 4, 4)), dma((4,)), dma((4,)),
            dma((4,)), dma((4,)), dma((2, 4, 2)), dma((2, 4, 2)), dma((16,)), dma((16,)),
            dma((2,)),
        ],
        compiler_params=pltpu.CompilerParams(
            collective_id=0, has_side_effects=True, vmem_limit_bytes=48 * 1024 * 1024),
    )(va, vb, panel_modes, fa, fbt, msq, mdf)
    elements = modal_stress.shape[1]
    st = jnp.pad(modal_stress.T, ((0, 0), (0, 2 * MH - M)))
    tile = 128
    return pl.pallas_call(
        stress_kernel,
        out_shape=jax.ShapeDtypeStruct((elements, 2, A8, 256), BF16),
        grid=(elements // tile,),
        in_specs=[
            pl.BlockSpec((tile, 2 * MH), lambda i: (i, 0)),
            pl.BlockSpec((8, 2, 4, MH, 128), lambda i: (0, 0, 0, 0, 0)),
        ],
        out_specs=pl.BlockSpec((tile, 2, A8, 256), lambda i: (i, 0, 0, 0)),
        scratch_shapes=[
            pltpu.VMEM((16, 2, MH, 256), BF16),
            pltpu.VMEM((tile, 16, 256), F32),
        ],
        compiler_params=pltpu.CompilerParams(vmem_limit_bytes=48 * 1024 * 1024),
    )(st, r)


def solution(mesh):
    in_specs = (
        P("pair", None, None, "zone"),
        P("pair", None, None, "zone"),
        P(None, "zone"),
        P(None, "zone"),
        P("pair"),
        P(),
        P(),
        P(),
    )
    out_specs = P("zone", None, "pair", None)
    return jax.shard_map(local, mesh=mesh, in_specs=in_specs, out_specs=out_specs, check_vma=False)
```

```python
import functools

import jax
import jax.numpy as jnp
from jax import lax
from jax.experimental import pallas as pl
from jax.experimental.pallas import tpu as pltpu
from jax.sharding import PartitionSpec as P

MESH = pl.DeviceIdType.MESH
F32 = jnp.float32
BF16 = jnp.bfloat16

A8 = 8
B32 = 32
KD = 1792
KT = KD // 128
M = 200
FM, FD = 264, 464
MH = 104
EVEN = ((0, 0), (0, 1), (2, 0), (2, 1))
ODD = ((1, 0), (3, 0), (1, 1), (3, 1))


def main_kernel(
    va, vb, modes_in, small_in,
    rhs,
    small, modes, r_in, vel, fas, msq, mdf, vf, uf, prs0, prs1, grid_f,
    tx_sib, rx_sib, tx_z, rx_z, tx_x, rx_x, resp,
    vel_ss, vel_rs, fa_ss, fa_rs, sib_ss, sib_rs, z_ss, z_rs, x_ss, x_rs,
    a_ss, a_rs, g_ss, g_rs, gs_ss, gs_rs, loc_sem,
):
    pair = lax.axis_index("pair")
    zone = lax.axis_index("zone")
    y, xl = pair // 2, pair % 2
    core, z, xh = zone % 2, (zone // 2) % 8, zone // 16

    def dev(dy=0, dx=0, dz=0, dh=0, dc=0):
        return (
            ((y + dy) % 4) * 2 + (xl + dx) % 2,
            (((xh + dh) % 2) * 8 + (z + dz + 8) % 8) * 2 + (core + dc) % 2,
        )

    cross = (y + core) % 2

    def group(j):
        dy = (1 - cross) * EVEN[j][0] + cross * ODD[j][0]
        dx = (1 - cross) * EVEN[j][1] + cross * ODD[j][1]
        return dy, dx

    def exchange_peer(j):
        dy, dx = group(j)
        return (((y + dy) % 4) * 2 + (xl + dx) % 2, (xh * 8 + z) * 2 + y % 2)

    crossed = cross == 1

    barrier = pltpu.get_barrier_semaphore()
    pair_peers = [(dy, dx) for dy in range(4) for dx in range(2) if (dy, dx) != (0, 0)]
    for dy, dx in pair_peers:
        pl.semaphore_signal(barrier, inc=1, device_id=dev(dy=dy, dx=dx), device_id_type=MESH)
    for kw in (dict(dc=1), dict(dz=1), dict(dz=-1), dict(dz=2), dict(dz=-2), dict(dh=1)):
        pl.semaphore_signal(barrier, inc=1, device_id=dev(**kw), device_id_type=MESH)

    @pl.when(crossed)
    def _():
        for j in range(4):
            pl.semaphore_signal(barrier, inc=1, device_id=exchange_peer(j), device_id_type=MESH)

    own_vel = pltpu.make_async_copy(va, vel.at[0], loc_sem.at[0])
    own_vel.start()
    own_modes = pltpu.make_async_copy(modes_in, modes, loc_sem.at[1])
    own_modes.start()
    own_small = pltpu.make_async_copy(small_in, small, loc_sem.at[2])
    own_small.start()
    pl.semaphore_wait(barrier, 13 + 4 * cross)

    def vel_copy(src, dst, k, to, half=None):
        s = va if src == 0 else vel.at[src] if half is None else vel.at[src, :, pl.ds(half, KD // 2)]
        d = vel.at[dst] if half is None else vel.at[dst, :, pl.ds(half, KD // 2)]
        return pltpu.make_async_remote_copy(
            src_ref=s, dst_ref=d, send_sem=vel_ss.at[k], recv_sem=vel_rs.at[k],
            device_id=to, device_id_type=MESH)

    c_x = vel_copy(0, 1, 0, dev(dx=1))
    c_yp = vel_copy(0, 6, 1, dev(dy=1))
    c_ym = vel_copy(0, 2, 2, dev(dy=3))
    c_xyp = vel_copy(1, 7, 3, dev(dy=1))
    c_xym = vel_copy(1, 3, 4, dev(dy=3))
    c_fyp = vel_copy(6, 4, 5, dev(dy=1), 0)
    c_fym = vel_copy(2, 4, 6, dev(dy=3), KD // 2)
    c_x2 = vel_copy(4, 5, 7, dev(dx=1), 0)
    c_x3 = vel_copy(4, 5, 8, dev(dx=1), KD // 2)
    c_yp.start()
    c_ym.start()
    c_x.start()
    own_small.wait()
    for a in range(A8):
        fas[0, a:a + 1, :] = jnp.full((1, 128), small[a], F32)
    fa_copies = []
    for n, (dy, dx) in enumerate(pair_peers):
        slot = 2 * ((4 - dy) % 4) + dx
        cp = pltpu.make_async_remote_copy(
            src_ref=fas.at[0], dst_ref=fas.at[slot], send_sem=fa_ss.at[n], recv_sem=fa_rs.at[n],
            device_id=dev(dy=dy, dx=dx), device_id_type=MESH)
        cp.start()
        fa_copies.append(cp)

    def zero_pad(n, _):
        grid_f[n // 4, 4 + n % 4, 96:104, :] = jnp.zeros((8, 128), F32)
        return 0

    lax.fori_loop(0, 20, zero_pad, 0)

    def mode_row(n, _):
        for h in range(2):
            f = small[FM + h * MH + n]
            msq[h, pl.ds(n, 1), :] = jnp.full((1, 128), f * f, F32)
            mdf[h, pl.ds(n, 1), :] = jnp.full((1, 128), 2.0 * small[FD + h * MH + n] * f, F32)
        return 0

    lax.fori_loop(0, 96, mode_row, 0)
    for n in range(96, 104):
        f = small[FM + n]
        msq[0, n:n + 1, :] = jnp.full((1, 128), f * f, F32)
        mdf[0, n:n + 1, :] = jnp.full((1, 128), 2.0 * small[FD + n] * f, F32)
    msq[1, 96:104, :] = jnp.ones((8, 128), F32)
    mdf[1, 96:104, :] = jnp.ones((8, 128), F32)

    def prep(kt, _):
        lanes = pl.ds(pl.multiple_of(kt * 128, 128), 128)
        for c in range(3):
            vr = vb[c * 64:c * 64 + 32, lanes].astype(F32)
            vi = vb[c * 64 + 32:c * 64 + 64, lanes].astype(F32)
            vf[kt, c * 3] = vr
            vf[kt, c * 3 + 1] = vi - vr
            vf[kt, c * 3 + 2] = vr + vi
        return 0

    lax.fori_loop(0, KT, prep, 0)

    def sib_copy(j):
        return pltpu.make_async_remote_copy(
            src_ref=tx_sib.at[j], dst_ref=rx_sib.at[j], send_sem=sib_ss.at[j], recv_sem=sib_rs.at[j],
            device_id=dev(dc=1), device_id_type=MESH)

    def mine(dx):
        return cross == dx

    def send_sibling(j, dx):
        @pl.when(jnp.logical_not(mine(dx)))
        def _():
            def one(t, _):
                tx_sib[j, t] = grid_f[4, t].astype(BF16)
                return 0

            lax.fori_loop(0, 8, one, 0)
            sib_copy(j).start()

    def z_copy(d, n, j):
        hop = (1, 2, 1, 2)[n]
        return pltpu.make_async_remote_copy(
            src_ref=tx_z.at[d, n, j], dst_ref=rx_z.at[d, n, j],
            send_sem=z_ss.at[d, n, j], recv_sem=z_rs.at[d, n, j],
            device_id=dev(dz=hop if d == 0 else -hop), device_id_type=MESH)

    def x_copy(j):
        return pltpu.make_async_remote_copy(
            src_ref=tx_x.at[j], dst_ref=rx_x.at[j], send_sem=x_ss.at[j], recv_sem=x_rs.at[j],
            device_id=dev(dh=1), device_id_type=MESH)

    def a_copy(j):
        return pltpu.make_async_remote_copy(
            src_ref=resp.at[j], dst_ref=r_in.at[z, y % 2, (y // 2) * 2 + xl],
            send_sem=a_ss.at[j], recv_sem=a_rs.at[j],
            device_id=exchange_peer(j), device_id_type=MESH)

    def origin(j):
        dy, dx = group(j)
        return ((y + 4 - dy) % 4 // 2) * 2 + (xl + dx) % 2

    def a_arrival(j):
        return pltpu.make_async_remote_copy(
            src_ref=resp.at[0], dst_ref=r_in.at[z, core, origin(j)],
            send_sem=a_ss.at[j], recv_sem=a_rs.at[j],
            device_id=dev(dc=1), device_id_type=MESH)

    def g_copy(d, far, j):
        back = 0 if far <= 2 else 2
        src = (z - back + 8) % 8 if d == 0 else (z + back) % 8
        hop = far - back
        part = r_in.at[src, core, origin(j)]
        return pltpu.make_async_remote_copy(
            src_ref=part, dst_ref=part, send_sem=g_ss.at[d, far - 1, j], recv_sem=g_rs.at[d, far - 1, j],
            device_id=dev(dz=hop if d == 0 else -hop), device_id_type=MESH)

    def g_arrival(d, far, j):
        src = (z - far + 8) % 8 if d == 0 else (z + far) % 8
        part = r_in.at[src, core, origin(j)]
        return pltpu.make_async_remote_copy(
            src_ref=part, dst_ref=part, send_sem=g_ss.at[d, far - 1, j], recv_sem=g_rs.at[d, far - 1, j],
            device_id=dev(dc=1), device_id_type=MESH)

    def sib_chunk(dz, j, own=True):
        if own:
            where = origin(j)
        else:
            other = 1 - cross
            dy = (1 - other) * EVEN[j][0] + other * ODD[j][0]
            dx = (1 - other) * EVEN[j][1] + other * ODD[j][1]
            where = ((y + 4 - dy) % 4 // 2) * 2 + (xl + dx) % 2
        part = r_in.at[(z + dz + 8) % 8, core if own else 1 - core, where]
        return pltpu.make_async_remote_copy(
            src_ref=part, dst_ref=part, send_sem=gs_ss.at[dz + 4, j], recv_sem=gs_rs.at[dz + 4, j],
            device_id=dev(dc=1), device_id_type=MESH)

    lane = lax.broadcasted_iota(jnp.int32, (1, 128), 1)
    second = (lane // 32) % 2 == 1
    sign = jnp.where(lane < 64, -1.0, 1.0).astype(F32)

    def part_for(j, t):
        return grid_f[j, t] + rx_sib[j, t].astype(F32)

    def far_side(d, j):
        return j % 2 == d

    def z_first(j):
        sib_copy(j).wait_recv()
        for n, dist in ((0, 3), (1, 4), (2, 1)):
            for d in range(2):
                if n == 1 and not far_side(d, j):
                    continue
                t = (z + dist) % 8 if d == 0 else (z - dist + 8) % 8
                tx_z[d, n, j] = part_for(j, t).astype(BF16)
                z_copy(d, n, j).start()

    def z_second(j):
        for d in range(2):
            t = (z + 2) % 8 if d == 0 else (z - 2 + 8) % 8
            value = part_for(j, t)
            for n in range(2):
                if n == 0 or far_side(d, j):
                    z_copy(d, n, j).wait_recv()
                    value = value + rx_z[d, n, j].astype(F32)
            tx_z[d, 3, j] = value.astype(BF16)
            z_copy(d, 3, j).start()

    def x_step(j):
        value = part_for(j, z)
        for n in (2, 3):
            for d in range(2):
                z_copy(d, n, j).wait_recv()
                value = value + rx_z[d, n, j].astype(F32)
        grid_f[j, z] = value
        tx_x[j] = value.astype(BF16)
        x_copy(j).start()

    def respond(j):
        if j == 0:
            for cp in fa_copies:
                cp.wait()
        zh, zl = z // 4, z % 4
        gy, gx = group(j)
        slot = 2 * gy + gx
        s2 = msq[zh]
        x_copy(j).wait_recv()
        f = grid_f[j, z] + rx_x[j].astype(F32)
        fb_row = jnp.zeros((1, 128), F32)
        for b in range(B32):
            fb_row = jnp.where(lane % B32 == b, small[A8 + pair * B32 + b], fb_row)
        w = jnp.where(second, fas[slot, pl.ds(zl * 2 + 1, 1), :], fas[slot, pl.ds(zl * 2, 1), :]) + fb_row
        t = s2 - w * w
        g = mdf[zh] * w
        inv = 1.0 / (t * t + g * g)
        re = s2 * t * inv
        im = -s2 * g * inv
        out = (re * f + im * (sign * pltpu.roll(f, 64, 1))).astype(BF16)
        if j == 0:
            @pl.when(crossed)
            def _():
                resp[j] = out
                a_copy(j).start()

            @pl.when(jnp.logical_not(crossed))
            def _():
                r_in[z, y % 2, (y // 2) * 2 + xl] = out
        else:
            resp[j] = out
            a_copy(j).start()

    def g_first(j):
        if j == 0:
            @pl.when(crossed)
            def _():
                a_arrival(0).wait_recv()
        else:
            a_arrival(j).wait_recv()
        for far in (2, 1):
            for d in range(2):
                g_copy(d, far, j).start()
        sib_chunk(0, j).start()

    def g_second(j):
        for d in range(2):
            g_arrival(d, 2, j).wait_recv()
            g_copy(d, 3, j).start()
            if far_side(d, j):
                g_copy(d, 4, j).start()
        for d in range(2):
            sib_chunk(2 if d else -2, j).start()
        for d in range(2):
            g_arrival(d, 1, j).wait_recv()
            sib_chunk(1 if d else -1, j).start()

    def g_last(j):
        for d in range(2):
            g_arrival(d, 3, j).wait_recv()
            sib_chunk(3 if d else -3, j).start()
        g_arrival(j % 2, 4, j).wait_recv()
        sib_chunk(-4, j).start()

    def arrange(dz):
        for j in range(4):
            sib_chunk(dz, j, own=False).wait_recv()
        zc = (z + dz + 8) % 8
        zh, zl = zc // 4, zc % 4
        low, even = lane < 64, (lane // 32) % 2 == 0

        def half(hp, _):
            b = [r_in[zc, i // 2, hp * 2 + i % 2].astype(F32) for i in range(4)]
            u = [None] * 4
            for i in range(2):
                u[i] = jnp.where(low, b[i], pltpu.roll(b[i + 2], 64, 1))
                u[i + 2] = jnp.where(low, pltpu.roll(b[i], 64, 1), b[i + 2])
            w = [None] * 4
            for i in (0, 2):
                w[i] = jnp.where(even, u[i], pltpu.roll(u[i + 1], 32, 1))
                w[i + 1] = jnp.where(even, pltpu.roll(u[i], 96, 1), u[i + 1])
            for g in range(4):
                idx = (g // 2) * 8 + zl * 2 + g % 2
                rhs[idx, zh, :, pl.ds(pl.multiple_of(hp * 128, 128), 128)] = w[g].astype(BF16)
            return 0

        lax.fori_loop(0, 2, half, 0)

    STAGES = (z_first, z_second, x_step, respond, g_first, g_second, g_last)

    def stage(j, k):
        STAGES[k](j)
        if j == 3 and k == 5:
            arrange(0)
        if j == 3 and k == 6:
            for dz in (1, -1, 2, -2):
                arrange(dz)

    WHEN = ((4, 6, 8, 9, 10, 11, 12), (6, 8, 9, 10, 11, 12, 13),
            (8, 9, 10, 11, 12, 13, 14), (10, 11, 12, 13, 14, 15, 16))

    def events(t):
        return [(j, WHEN[j].index(t)) for j in (3, 2, 1, 0) if t in WHEN[j]]

    def forces(prs, h, dst):
        f = lax.dot_general(
            modes[...], prs[pl.ds(pl.multiple_of(h * 256, 256), 256), :], (((1,), (1,)), ((), ())),
            preferred_element_type=F32)
        for n in range(2):
            grid_f[dst, 2 * h + n] = f[0:104, n * 128:n * 128 + 128]
            grid_f[dst, 4 + 2 * h + n, 0:96] = f[104:200, n * 128:n * 128 + 128]

    def pressure(prs, slot, kt, k):
        lanes = pl.ds(pl.multiple_of(kt * 128, 128), 128)
        for c in range(3):
            both = vel[slot, c * 16:c * 16 + 16, lanes].astype(F32)
            ur, ui = both[0:8] * -0.5, both[8:16] * -0.5
            uf[k, c * 24:c * 24 + 8] = ur
            uf[k, c * 24 + 8:c * 24 + 16] = ui
            uf[k, c * 24 + 16:c * 24 + 24] = ur + ui
        for half in range(2):
            v = [vf[kt, n, half * 16:half * 16 + 16, :] for n in range(9)]
            for a in range(A8):
                row = (a // 2) * 128 + (a % 2) * 32 + half * 16
                k1 = k2 = k3 = None
                for c in range(3):
                    ur = uf[k, c * 24 + a:c * 24 + a + 1, :]
                    ui = uf[k, c * 24 + 8 + a:c * 24 + 8 + a + 1, :]
                    us = uf[k, c * 24 + 16 + a:c * 24 + 16 + a + 1, :]
                    t1, t2, t3 = v[c * 3] * us, v[c * 3 + 1] * ur, v[c * 3 + 2] * ui
                    k1 = t1 if k1 is None else k1 + t1
                    k2 = t2 if k2 is None else k2 + t2
                    k3 = t3 if k3 is None else k3 + t3
                prs[row:row + 16, lanes] = (k1 - k3).astype(BF16)
                prs[row + 64:row + 80, lanes] = (k1 + k2).astype(BF16)

    own_modes.wait()
    own_vel.wait()
    bufs = (prs0, prs1)

    def double_block(j, _):
        slots = (j % 2 + 4 * (j // 2), 2 + 4 * (j % 2) + j // 2)
        for dx in range(2):
            slot = slots[dx]
            if dx == 0:
                @pl.when(j == 3)
                def _():
                    c_x2.wait_recv()
                    c_x3.wait_recv()
            else:
                @pl.when(j == 0)
                def _():
                    c_yp.wait_recv()
                    c_fyp.start()
                    c_ym.wait_recv()
                    c_fym.start()
                    c_x.wait_recv()
                    c_xym.start()
                    c_xyp.start()

                @pl.when(j == 1)
                def _():
                    c_fyp.wait_recv()
                    c_x2.start()
                    c_fym.wait_recv()
                    c_x3.start()

                @pl.when(j == 2)
                def _():
                    c_xym.wait_recv()

                @pl.when(j == 3)
                def _():
                    c_xyp.wait_recv()

            @pl.when(j >= 1)
            def _():
                send_sibling(j - 1, dx)

            for jj in range(4):
                for t in events(2 * jj + dx):
                    @pl.when(j == jj)
                    def _():
                        stage(*t)

            if dx == 0:
                dst = jnp.where(jnp.logical_and(mine(1), j >= 1), jnp.maximum(j - 1, 0), 4)
            else:
                dst = jnp.where(mine(0), j, 4)

            def half(h, _):
                forces(bufs[1 - dx], h, dst)
                for k in range(7):
                    pressure(bufs[dx], slot, h * 7 + k, k)
                return 0

            lax.fori_loop(0, 2, half, 0)
        return 0

    lax.fori_loop(0, 4, double_block, 0)

    send_sibling(3, 0)
    last = jnp.where(mine(1), 3, 4)

    def last_half(h, _):
        forces(prs1, h, last)
        return 0

    lax.fori_loop(0, 2, last_half, 0)
    send_sibling(3, 1)
    for t in range(8, 17):
        for j, k in events(t):
            stage(j, k)
    for dz in (3, -3, -4):
        arrange(dz)

    for cp in (c_x, c_yp, c_ym, c_xyp, c_xym, c_fyp, c_fym, c_x2, c_x3):
        cp.wait_send()

    def drain(j, _):
        sib_copy(j).wait_send()
        x_copy(j).wait_send()
        return 0

    lax.fori_loop(0, 4, drain, 0)
    for j in range(4):
        for n in range(4):
            for d in range(2):
                if n != 1 or far_side(d, j):
                    z_copy(d, n, j).wait_send()
    for j in range(1, 4):
        a_copy(j).wait_send()

    @pl.when(crossed)
    def _():
        a_copy(0).wait_send()

    for j in range(4):
        for far in range(1, 5):
            for d in range(2):
                if far < 4 or far_side(d, j):
                    g_copy(d, far, j).wait_send()
        for dz in range(-4, 4):
            sib_chunk(dz, j).wait_send()


def stress_kernel(ms, rhs, out, acc):
    for ra in range(16):
        r = rhs[ra].reshape(2 * MH, 256)[:M]
        acc[:, ra, :] = lax.dot_general(
            ms[...], r, (((0,), (0,)), ((), ())), preferred_element_type=F32)
    out[...] = acc[...].reshape(out.shape).astype(BF16)


def local(vel_a, vel_b, panel_modes, modal_stress, freq_a, freq_b, mode_freq, damping):
    va = jnp.transpose(vel_a, (2, 1, 0, 3)).reshape(48, KD)
    vb = jnp.transpose(vel_b, (2, 1, 0, 3)).reshape(192, KD)
    small = jnp.concatenate([freq_a, freq_b, mode_freq, damping])
    vm = pl.BlockSpec(memory_space=pltpu.VMEM)
    hbm = pl.BlockSpec(memory_space=pltpu.HBM)
    dma = pltpu.SemaphoreType.DMA
    r = pl.pallas_call(
        main_kernel,
        out_shape=jax.ShapeDtypeStruct((16, 2, MH, 256), BF16),
        in_specs=[vm, vm, hbm, hbm],
        out_specs=vm,
        scratch_shapes=[
            pltpu.SMEM((A8 + 256 + 2 * M,), F32),
            pltpu.VMEM((M, KD), BF16),
            pltpu.VMEM((8, 2, 4, MH, 128), BF16),
            pltpu.VMEM((8, 48, KD), BF16),
            pltpu.VMEM((8, A8, 128), F32),
            pltpu.VMEM((2, MH, 128), F32),
            pltpu.VMEM((2, MH, 128), F32),
            pltpu.VMEM((KT, 9, B32, 128), F32),
            pltpu.VMEM((7, 72, 128), F32),
            pltpu.VMEM((512, KD), BF16),
            pltpu.VMEM((512, KD), BF16),
            pltpu.VMEM((5, 8, MH, 128), F32),
            pltpu.VMEM((4, 8, MH, 128), BF16),
            pltpu.VMEM((4, 8, MH, 128), BF16),
            pltpu.VMEM((2, 4, 4, MH, 128), BF16),
            pltpu.VMEM((2, 4, 4, MH, 128), BF16),
            pltpu.VMEM((4, MH, 128), BF16),
            pltpu.VMEM((4, MH, 128), BF16),
            pltpu.VMEM((4, MH, 128), BF16),
            dma((9,)), dma((9,)), dma((7,)), dma((7,)), dma((4,)), dma((4,)),
            dma((2, 4, 4)), dma((2, 4, 4)), dma((4,)), dma((4,)),
            dma((4,)), dma((4,)), dma((2, 4, 4)), dma((2, 4, 4)), dma((8, 4)), dma((8, 4)),
            dma((3,)),
        ],
        compiler_params=pltpu.CompilerParams(
            collective_id=0, has_side_effects=True, vmem_limit_bytes=48 * 1024 * 1024),
    )(va, vb, panel_modes, small)
    elements = modal_stress.shape[1]
    tile = 128
    return pl.pallas_call(
        stress_kernel,
        out_shape=jax.ShapeDtypeStruct((elements, 2, A8, 256), BF16),
        grid=(elements // tile,),
        in_specs=[
            pl.BlockSpec((M, tile), lambda i: (0, i)),
            pl.BlockSpec((16, 2, MH, 256), lambda i: (0, 0, 0, 0)),
        ],
        out_specs=pl.BlockSpec((tile, 2, A8, 256), lambda i: (i, 0, 0, 0)),
        scratch_shapes=[pltpu.VMEM((tile, 16, 256), F32)],
        compiler_params=pltpu.CompilerParams(vmem_limit_bytes=48 * 1024 * 1024),
    )(modal_stress, r)


def solution(mesh):
    in_specs = (
        P("pair", None, None, "zone"),
        P("pair", None, None, "zone"),
        P(None, "zone"),
        P(None, "zone"),
        P("pair"),
        P(),
        P(),
        P(),
    )
    out_specs = P("zone", None, "pair", None)
    return jax.shard_map(local, mesh=mesh, in_specs=in_specs, out_specs=out_specs, check_vma=False)
```

```python
import functools

import jax
import jax.numpy as jnp
from jax import lax
from jax.experimental import pallas as pl
from jax.experimental.pallas import tpu as pltpu
from jax.sharding import PartitionSpec as P

MESH = pl.DeviceIdType.MESH
F32 = jnp.float32
BF16 = jnp.bfloat16

A8 = 8
B32 = 32
KD = 1792
KT = KD // 128
M = 200
FM, FD = 264, 464
MH = 104
EVEN = ((0, 0), (0, 1), (2, 0), (2, 1))
ODD = ((1, 0), (3, 0), (1, 1), (3, 1))


def main_kernel(
    va, vb, modes_in, small_in,
    rhs,
    small, modes, r_in, vel, msq, mdf, vf, uf, prs0, prs1, grid_f,
    tx_sib, rx_sib, tx_z, rx_z, tx_a, rx_a,
    vel_ss, vel_rs, sib_ss, sib_rs, z_ss, z_rs,
    a_ss, a_rs, g_ss, g_rs, gs_ss, gs_rs, loc_sem,
):
    pair = lax.axis_index("pair")
    zone = lax.axis_index("zone")
    y, xl = pair // 2, pair % 2
    core, z, xh = zone % 2, (zone // 2) % 8, zone // 16

    def dev(dy=0, dx=0, dz=0, dh=0, dc=0):
        return (
            ((y + dy) % 4) * 2 + (xl + dx) % 2,
            (((xh + dh) % 2) * 8 + (z + dz + 8) % 8) * 2 + (core + dc) % 2,
        )

    cross = (y + core) % 2

    def group(j):
        dy = (1 - cross) * EVEN[j][0] + cross * ODD[j][0]
        dx = (1 - cross) * EVEN[j][1] + cross * ODD[j][1]
        return dy, dx

    def exchange_peer(j, dh=0):
        dy, dx = group(j)
        return (((y + dy) % 4) * 2 + (xl + dx) % 2, (((xh + dh) % 2) * 8 + z) * 2 + y % 2)

    crossed = cross == 1

    barrier = pltpu.get_barrier_semaphore()
    pair_peers = [(dy, dx) for dy in range(4) for dx in range(2) if (dy, dx) != (0, 0)]
    for dy, dx in pair_peers:
        pl.semaphore_signal(barrier, inc=1, device_id=dev(dy=dy, dx=dx), device_id_type=MESH)
    for kw in (dict(dc=1), dict(dz=1), dict(dz=-1), dict(dz=2), dict(dz=-2)):
        pl.semaphore_signal(barrier, inc=1, device_id=dev(**kw), device_id_type=MESH)

    for j in range(4):
        pl.semaphore_signal(barrier, inc=1, device_id=exchange_peer(j, 1), device_id_type=MESH)

    @pl.when(crossed)
    def _():
        for j in range(4):
            pl.semaphore_signal(barrier, inc=1, device_id=exchange_peer(j), device_id_type=MESH)

    own_vel = pltpu.make_async_copy(va, vel.at[0], loc_sem.at[0])
    own_vel.start()
    own_modes = pltpu.make_async_copy(modes_in, modes, loc_sem.at[1])
    own_modes.start()
    own_small = pltpu.make_async_copy(small_in, small, loc_sem.at[2])
    own_small.start()
    pl.semaphore_wait(barrier, 16 + 4 * cross)

    def vel_copy(src, dst, k, to, half=None):
        s = va if src == 0 else vel.at[src] if half is None else vel.at[src, :, pl.ds(half, KD // 2)]
        d = vel.at[dst] if half is None else vel.at[dst, :, pl.ds(half, KD // 2)]
        return pltpu.make_async_remote_copy(
            src_ref=s, dst_ref=d, send_sem=vel_ss.at[k], recv_sem=vel_rs.at[k],
            device_id=to, device_id_type=MESH)

    c_x = vel_copy(0, 1, 0, dev(dx=1))
    c_yp = vel_copy(0, 6, 1, dev(dy=1))
    c_ym = vel_copy(0, 2, 2, dev(dy=3))
    c_xyp = vel_copy(1, 7, 3, dev(dy=1))
    c_xym = vel_copy(1, 3, 4, dev(dy=3))
    c_fyp = vel_copy(6, 4, 5, dev(dy=1), 0)
    c_fym = vel_copy(2, 4, 6, dev(dy=3), KD // 2)
    c_x2 = vel_copy(4, 5, 7, dev(dx=1), 0)
    c_x3 = vel_copy(4, 5, 8, dev(dx=1), KD // 2)
    c_yp.start()
    c_ym.start()
    c_x.start()
    own_small.wait()
    def zero_pad(n, _):
        grid_f[n // 4, 4 + n % 4, 96:104, :] = jnp.zeros((8, 128), F32)
        return 0

    lax.fori_loop(0, 20, zero_pad, 0)

    def mode_row(n, _):
        for h in range(2):
            f = small[FM + h * MH + n]
            msq[h, pl.ds(n, 1), :] = jnp.full((1, 128), f * f, F32)
            mdf[h, pl.ds(n, 1), :] = jnp.full((1, 128), 2.0 * small[FD + h * MH + n] * f, F32)
        return 0

    lax.fori_loop(0, 96, mode_row, 0)
    for n in range(96, 104):
        f = small[FM + n]
        msq[0, n:n + 1, :] = jnp.full((1, 128), f * f, F32)
        mdf[0, n:n + 1, :] = jnp.full((1, 128), 2.0 * small[FD + n] * f, F32)
    msq[1, 96:104, :] = jnp.ones((8, 128), F32)
    mdf[1, 96:104, :] = jnp.ones((8, 128), F32)

    def prep(kt, _):
        lanes = pl.ds(pl.multiple_of(kt * 128, 128), 128)
        for c in range(3):
            vr = vb[c * 64:c * 64 + 32, lanes].astype(F32)
            vi = vb[c * 64 + 32:c * 64 + 64, lanes].astype(F32)
            vf[kt, c * 3] = vr
            vf[kt, c * 3 + 1] = vi - vr
            vf[kt, c * 3 + 2] = vr + vi
        return 0

    lax.fori_loop(0, KT, prep, 0)

    def sib_copy(j):
        return pltpu.make_async_remote_copy(
            src_ref=tx_sib.at[j], dst_ref=rx_sib.at[j], send_sem=sib_ss.at[j], recv_sem=sib_rs.at[j],
            device_id=dev(dc=1), device_id_type=MESH)

    def mine(dx):
        return cross == dx

    def send_sibling(j, dx):
        @pl.when(jnp.logical_not(mine(dx)))
        def _():
            def one(t, _):
                tx_sib[j, t] = grid_f[4, t].astype(BF16)
                return 0

            lax.fori_loop(0, 8, one, 0)
            sib_copy(j).start()

    def z_copy(d, n, j):
        hop = (1, 2, 1, 2)[n]
        return pltpu.make_async_remote_copy(
            src_ref=tx_z.at[d, n, j], dst_ref=rx_z.at[d, n, j],
            send_sem=z_ss.at[d, n, j], recv_sem=z_rs.at[d, n, j],
            device_id=dev(dz=hop if d == 0 else -hop), device_id_type=MESH)

    def a_copy(n, j):
        return pltpu.make_async_remote_copy(
            src_ref=tx_a.at[j], dst_ref=rx_a.at[n, j],
            send_sem=a_ss.at[n, j], recv_sem=a_rs.at[n, j],
            device_id=exchange_peer(j, n), device_id_type=MESH)

    def origin(j):
        dy, dx = group(j)
        return ((y + 4 - dy) % 4 // 2) * 2 + (xl + dx) % 2

    def g_copy(d, far, j):
        back = 0 if far <= 2 else 2
        src = (z - back + 8) % 8 if d == 0 else (z + back) % 8
        hop = far - back
        part = r_in.at[src, core, origin(j)]
        return pltpu.make_async_remote_copy(
            src_ref=part, dst_ref=part, send_sem=g_ss.at[d, far - 1, j], recv_sem=g_rs.at[d, far - 1, j],
            device_id=dev(dz=hop if d == 0 else -hop), device_id_type=MESH)

    def g_arrival(d, far, j):
        src = (z - far + 8) % 8 if d == 0 else (z + far) % 8
        part = r_in.at[src, core, origin(j)]
        return pltpu.make_async_remote_copy(
            src_ref=part, dst_ref=part, send_sem=g_ss.at[d, far - 1, j], recv_sem=g_rs.at[d, far - 1, j],
            device_id=dev(dc=1), device_id_type=MESH)

    def sib_chunk(dz, j, own=True):
        if own:
            where = origin(j)
        else:
            other = 1 - cross
            dy = (1 - other) * EVEN[j][0] + other * ODD[j][0]
            dx = (1 - other) * EVEN[j][1] + other * ODD[j][1]
            where = ((y + 4 - dy) % 4 // 2) * 2 + (xl + dx) % 2
        part = r_in.at[(z + dz + 8) % 8, core if own else 1 - core, where]
        return pltpu.make_async_remote_copy(
            src_ref=part, dst_ref=part, send_sem=gs_ss.at[dz + 4, j], recv_sem=gs_rs.at[dz + 4, j],
            device_id=dev(dc=1), device_id_type=MESH)

    lane = lax.broadcasted_iota(jnp.int32, (1, 128), 1)
    second = (lane // 32) % 2 == 1
    sign = jnp.where(lane < 64, -1.0, 1.0).astype(F32)

    def part_for(j, t):
        return grid_f[j, t] + rx_sib[j, t].astype(F32)

    def far_side(d, j):
        return j % 2 == d

    def z_first(j):
        sib_copy(j).wait_recv()
        for n, dist in ((0, 3), (1, 4), (2, 1)):
            for d in range(2):
                if n == 1 and not far_side(d, j):
                    continue
                t = (z + dist) % 8 if d == 0 else (z - dist + 8) % 8
                tx_z[d, n, j] = part_for(j, t).astype(BF16)
                z_copy(d, n, j).start()

    def z_second(j):
        for d in range(2):
            t = (z + 2) % 8 if d == 0 else (z - 2 + 8) % 8
            value = part_for(j, t)
            for n in range(2):
                if n == 0 or far_side(d, j):
                    z_copy(d, n, j).wait_recv()
                    value = value + rx_z[d, n, j].astype(F32)
            tx_z[d, 3, j] = value.astype(BF16)
            z_copy(d, 3, j).start()

    def exchange(j):
        value = part_for(j, z)
        for n in (2, 3):
            for d in range(2):
                z_copy(d, n, j).wait_recv()
                value = value + rx_z[d, n, j].astype(F32)
        value = value.astype(BF16)
        tx_a[j] = value
        a_copy(1, j).start()
        if j == 0:
            @pl.when(crossed)
            def _():
                a_copy(0, 0).start()

            @pl.when(jnp.logical_not(crossed))
            def _():
                rx_a[0, 0] = value
        else:
            a_copy(0, j).start()

    def respond(j):
        zh, zl = z // 4, z % 4
        gy, gx = group(j)
        other = ((y + 4 - gy) % 4) * 2 + (xl + gx) % 2
        w = jnp.where(second, small[zl * 2 + 1], small[zl * 2])
        for b in range(B32):
            w = jnp.where(lane % B32 == b, w + small[A8 + other * B32 + b], w)
        s2 = msq[zh]
        t = s2 - w * w
        g = mdf[zh] * w
        inv = 1.0 / (t * t + g * g)
        re = s2 * t * inv
        im = -s2 * g * inv * sign
        if j == 0:
            @pl.when(crossed)
            def _():
                a_copy(0, 0).wait_recv()
        else:
            a_copy(0, j).wait_recv()
        a_copy(1, j).wait_recv()
        f = rx_a[0, j].astype(F32) + rx_a[1, j].astype(F32)
        r_in[z, core, origin(j)] = (re * f + im * pltpu.roll(f, 64, 1)).astype(BF16)
        for far in (2, 1):
            for d in range(2):
                g_copy(d, far, j).start()
        sib_chunk(0, j).start()

    def g_second(j):
        for d in range(2):
            g_arrival(d, 2, j).wait_recv()
            g_copy(d, 3, j).start()
            if far_side(d, j):
                g_copy(d, 4, j).start()
        for d in range(2):
            sib_chunk(2 if d else -2, j).start()
        for d in range(2):
            g_arrival(d, 1, j).wait_recv()
            sib_chunk(1 if d else -1, j).start()

    def g_last(j):
        for d in range(2):
            g_arrival(d, 3, j).wait_recv()
            sib_chunk(3 if d else -3, j).start()
        g_arrival(j % 2, 4, j).wait_recv()
        sib_chunk(-4, j).start()

    def arrange(dz):
        for j in range(4):
            sib_chunk(dz, j, own=False).wait_recv()
        zc = (z + dz + 8) % 8
        zh, zl = zc // 4, zc % 4
        low, even = lane < 64, (lane // 32) % 2 == 0

        def half(hp, _):
            b = [r_in[zc, i // 2, hp * 2 + i % 2].astype(F32) for i in range(4)]
            u = [None] * 4
            for i in range(2):
                u[i] = jnp.where(low, b[i], pltpu.roll(b[i + 2], 64, 1))
                u[i + 2] = jnp.where(low, pltpu.roll(b[i], 64, 1), b[i + 2])
            w = [None] * 4
            for i in (0, 2):
                w[i] = jnp.where(even, u[i], pltpu.roll(u[i + 1], 32, 1))
                w[i + 1] = jnp.where(even, pltpu.roll(u[i], 96, 1), u[i + 1])
            for g in range(4):
                idx = (g // 2) * 8 + zl * 2 + g % 2
                rhs[idx, zh, :, pl.ds(pl.multiple_of(hp * 128, 128), 128)] = w[g].astype(BF16)
            return 0

        lax.fori_loop(0, 2, half, 0)

    STAGES = (z_first, z_second, exchange, respond, g_second, g_last)

    def stage(j, k):
        STAGES[k](j)
        if j == 3 and k == 4:
            arrange(0)
        if j == 3 and k == 5:
            for dz in (1, -1, 2, -2):
                arrange(dz)

    WHEN = ((4, 6, 8, 9, 10, 11), (6, 8, 9, 10, 11, 12),
            (8, 9, 10, 11, 12, 13), (10, 11, 12, 13, 14, 15))

    def events(t):
        return [(j, WHEN[j].index(t)) for j in (3, 2, 1, 0) if t in WHEN[j]]

    def forces(prs, h, dst):
        f = lax.dot_general(
            modes[...], prs[pl.ds(pl.multiple_of(h * 256, 256), 256), :], (((1,), (1,)), ((), ())),
            preferred_element_type=F32)
        for n in range(2):
            grid_f[dst, 2 * h + n] = f[0:104, n * 128:n * 128 + 128]
            grid_f[dst, 4 + 2 * h + n, 0:96] = f[104:200, n * 128:n * 128 + 128]

    def pressure(prs, slot, kt, k):
        lanes = pl.ds(pl.multiple_of(kt * 128, 128), 128)
        for c in range(3):
            both = vel[slot, c * 16:c * 16 + 16, lanes].astype(F32)
            ur, ui = both[0:8] * -0.5, both[8:16] * -0.5
            uf[k, c * 24:c * 24 + 8] = ur
            uf[k, c * 24 + 8:c * 24 + 16] = ui
            uf[k, c * 24 + 16:c * 24 + 24] = ur + ui
        for half in range(2):
            v = [vf[kt, n, half * 16:half * 16 + 16, :] for n in range(9)]
            for a in range(A8):
                row = (a // 2) * 128 + (a % 2) * 32 + half * 16
                k1 = k2 = k3 = None
                for c in range(3):
                    ur = uf[k, c * 24 + a:c * 24 + a + 1, :]
                    ui = uf[k, c * 24 + 8 + a:c * 24 + 8 + a + 1, :]
                    us = uf[k, c * 24 + 16 + a:c * 24 + 16 + a + 1, :]
                    t1, t2, t3 = v[c * 3] * us, v[c * 3 + 1] * ur, v[c * 3 + 2] * ui
                    k1 = t1 if k1 is None else k1 + t1
                    k2 = t2 if k2 is None else k2 + t2
                    k3 = t3 if k3 is None else k3 + t3
                prs[row:row + 16, lanes] = (k1 - k3).astype(BF16)
                prs[row + 64:row + 80, lanes] = (k1 + k2).astype(BF16)

    own_modes.wait()
    own_vel.wait()
    bufs = (prs0, prs1)

    def double_block(j, _):
        slots = (j % 2 + 4 * (j // 2), 2 + 4 * (j % 2) + j // 2)
        for dx in range(2):
            slot = slots[dx]
            if dx == 0:
                @pl.when(j == 3)
                def _():
                    c_x2.wait_recv()
                    c_x3.wait_recv()
            else:
                @pl.when(j == 0)
                def _():
                    c_yp.wait_recv()
                    c_fyp.start()
                    c_ym.wait_recv()
                    c_fym.start()
                    c_x.wait_recv()
                    c_xym.start()
                    c_xyp.start()

                @pl.when(j == 1)
                def _():
                    c_fyp.wait_recv()
                    c_x2.start()
                    c_fym.wait_recv()
                    c_x3.start()

                @pl.when(j == 2)
                def _():
                    c_xym.wait_recv()

                @pl.when(j == 3)
                def _():
                    c_xyp.wait_recv()

            @pl.when(j >= 1)
            def _():
                send_sibling(j - 1, dx)

            for jj in range(4):
                for t in events(2 * jj + dx):
                    @pl.when(j == jj)
                    def _():
                        stage(*t)

            if dx == 0:
                dst = jnp.where(jnp.logical_and(mine(1), j >= 1), jnp.maximum(j - 1, 0), 4)
            else:
                dst = jnp.where(mine(0), j, 4)

            def half(h, _):
                forces(bufs[1 - dx], h, dst)
                for k in range(7):
                    pressure(bufs[dx], slot, h * 7 + k, k)
                return 0

            lax.fori_loop(0, 2, half, 0)
        return 0

    lax.fori_loop(0, 4, double_block, 0)

    send_sibling(3, 0)
    last = jnp.where(mine(1), 3, 4)

    def last_half(h, _):
        forces(prs1, h, last)
        return 0

    lax.fori_loop(0, 2, last_half, 0)
    send_sibling(3, 1)
    for t in range(8, 16):
        for j, k in events(t):
            stage(j, k)
    for dz in (3, -3, -4):
        arrange(dz)

    for cp in (c_x, c_yp, c_ym, c_xyp, c_xym, c_fyp, c_fym, c_x2, c_x3):
        cp.wait_send()

    def drain(j, _):
        sib_copy(j).wait_send()
        return 0

    lax.fori_loop(0, 4, drain, 0)
    for j in range(4):
        for n in range(4):
            for d in range(2):
                if n != 1 or far_side(d, j):
                    z_copy(d, n, j).wait_send()
    for j in range(1, 4):
        a_copy(0, j).wait_send()
    for j in range(4):
        a_copy(1, j).wait_send()

    @pl.when(crossed)
    def _():
        a_copy(0, 0).wait_send()

    for j in range(4):
        for far in range(1, 5):
            for d in range(2):
                if far < 4 or far_side(d, j):
                    g_copy(d, far, j).wait_send()
        for dz in range(-4, 4):
            sib_chunk(dz, j).wait_send()


def stress_kernel(ms, rhs, out, acc):
    count = out.shape[0]
    lhs = ms[...].T
    for ra in range(16):
        r = rhs[ra].reshape(2 * MH, 256)[:M]
        acc[ra] = lax.dot_general(
            lhs, r, (((1,), (0,)), ((), ())), preferred_element_type=F32).astype(BF16)
    to = lax.broadcasted_iota(jnp.int32, (128, 128), 0)
    of = lax.broadcasted_iota(jnp.int32, (128, 128), 1)
    swap = jnp.where((to % 8 == of // 16) & (to // 8 == of % 16), 1.0, 0.0).astype(BF16)
    for r_ in range(2):
        for e in range(0, count, 16):
            rows = jnp.concatenate([acc[r_ * 8 + a, e:e + 16, :] for a in range(A8)], 0)
            turned = lax.dot_general(swap, rows, (((1,), (0,)), ((), ())), preferred_element_type=F32)
            out[e:e + 16, r_] = turned.astype(BF16).reshape(16, A8, 256)


def local(vel_a, vel_b, panel_modes, modal_stress, freq_a, freq_b, mode_freq, damping):
    va = jnp.transpose(vel_a, (2, 1, 0, 3)).reshape(48, KD)
    vb = jnp.transpose(vel_b, (2, 1, 0, 3)).reshape(192, KD)
    small = jnp.concatenate([freq_a, freq_b, mode_freq, damping])
    vm = pl.BlockSpec(memory_space=pltpu.VMEM)
    hbm = pl.BlockSpec(memory_space=pltpu.HBM)
    dma = pltpu.SemaphoreType.DMA
    r = pl.pallas_call(
        main_kernel,
        out_shape=jax.ShapeDtypeStruct((16, 2, MH, 256), BF16),
        in_specs=[vm, vm, hbm, hbm],
        out_specs=vm,
        scratch_shapes=[
            pltpu.SMEM((A8 + 256 + 2 * M,), F32),
            pltpu.VMEM((M, KD), BF16),
            pltpu.VMEM((8, 2, 4, MH, 128), BF16),
            pltpu.VMEM((8, 48, KD), BF16),
            pltpu.VMEM((2, MH, 128), F32),
            pltpu.VMEM((2, MH, 128), F32),
            pltpu.VMEM((KT, 9, B32, 128), F32),
            pltpu.VMEM((7, 72, 128), F32),
            pltpu.VMEM((512, KD), BF16),
            pltpu.VMEM((512, KD), BF16),
            pltpu.VMEM((5, 8, MH, 128), F32),
            pltpu.VMEM((4, 8, MH, 128), BF16),
            pltpu.VMEM((4, 8, MH, 128), BF16),
            pltpu.VMEM((2, 4, 4, MH, 128), BF16),
            pltpu.VMEM((2, 4, 4, MH, 128), BF16),
            pltpu.VMEM((4, MH, 128), BF16),
            pltpu.VMEM((2, 4, MH, 128), BF16),
            dma((9,)), dma((9,)), dma((4,)), dma((4,)),
            dma((2, 4, 4)), dma((2, 4, 4)),
            dma((2, 4)), dma((2, 4)), dma((2, 4, 4)), dma((2, 4, 4)), dma((8, 4)), dma((8, 4)),
            dma((3,)),
        ],
        compiler_params=pltpu.CompilerParams(
            collective_id=0, has_side_effects=True, vmem_limit_bytes=48 * 1024 * 1024),
    )(va, vb, panel_modes, small)
    elements = modal_stress.shape[1]
    tile = 256
    return pl.pallas_call(
        stress_kernel,
        out_shape=jax.ShapeDtypeStruct((elements, 2, A8, 256), BF16),
        grid=(elements // tile,),
        in_specs=[
            pl.BlockSpec((M, tile), lambda i: (0, i)),
            pl.BlockSpec((16, 2, MH, 256), lambda i: (0, 0, 0, 0)),
        ],
        out_specs=pl.BlockSpec((tile, 2, A8, 256), lambda i: (i, 0, 0, 0)),
        scratch_shapes=[pltpu.VMEM((16, tile, 256), BF16)],
        compiler_params=pltpu.CompilerParams(vmem_limit_bytes=48 * 1024 * 1024),
    )(modal_stress, r)


def solution(mesh):
    in_specs = (
        P("pair", None, None, "zone"),
        P("pair", None, None, "zone"),
        P(None, "zone"),
        P(None, "zone"),
        P("pair"),
        P(),
        P(),
        P(),
    )
    out_specs = P("zone", None, "pair", None)
    return jax.shard_map(local, mesh=mesh, in_specs=in_specs, out_specs=out_specs, check_vma=False)
```

```python
import functools

import jax
import jax.numpy as jnp
from jax import lax
from jax.experimental import pallas as pl
from jax.experimental.pallas import tpu as pltpu
from jax.sharding import PartitionSpec as P

MESH = pl.DeviceIdType.MESH
F32 = jnp.float32
BF16 = jnp.bfloat16

A8 = 8
B32 = 32
KD = 1792
KT = KD // 128
M = 200
FM, FD = 264, 464
MH = 104
EVEN = ((0, 0), (0, 1), (2, 0), (2, 1))
ODD = ((1, 0), (3, 0), (1, 1), (3, 1))


def main_kernel(
    va, vb, modes_in, small_in,
    rhs,
    small, modes, r_in, vel, msq, mdf, vf, uf, prs, grid_f,
    tx_sib, rx_sib, tx_z, rx_z, tx_a, rx_a,
    vel_ss, vel_rs, sib_ss, sib_rs, z_ss, z_rs,
    a_ss, a_rs, g_ss, g_rs, gs_ss, gs_rs, loc_sem,
):
    pair = lax.axis_index("pair")
    zone = lax.axis_index("zone")
    y, xl = pair // 2, pair % 2
    core, z, xh = zone % 2, (zone // 2) % 8, zone // 16

    def dev(dy=0, dx=0, dz=0, dh=0, dc=0):
        return (
            ((y + dy) % 4) * 2 + (xl + dx) % 2,
            (((xh + dh) % 2) * 8 + (z + dz + 8) % 8) * 2 + (core + dc) % 2,
        )

    cross = (y + core) % 2

    def group(j):
        dy = (1 - cross) * EVEN[j][0] + cross * ODD[j][0]
        dx = (1 - cross) * EVEN[j][1] + cross * ODD[j][1]
        return dy, dx

    def exchange_peer(j, dh=0):
        dy, dx = group(j)
        return (((y + dy) % 4) * 2 + (xl + dx) % 2, (((xh + dh) % 2) * 8 + z) * 2 + y % 2)

    crossed = cross == 1

    barrier = pltpu.get_barrier_semaphore()
    pair_peers = [(dy, dx) for dy in range(4) for dx in range(2) if (dy, dx) != (0, 0)]
    for dy, dx in pair_peers:
        pl.semaphore_signal(barrier, inc=1, device_id=dev(dy=dy, dx=dx), device_id_type=MESH)
    for kw in (dict(dc=1), dict(dz=1), dict(dz=-1), dict(dz=2), dict(dz=-2)):
        pl.semaphore_signal(barrier, inc=1, device_id=dev(**kw), device_id_type=MESH)

    for j in range(4):
        pl.semaphore_signal(barrier, inc=1, device_id=exchange_peer(j, 1), device_id_type=MESH)

    @pl.when(crossed)
    def _():
        for j in range(4):
            pl.semaphore_signal(barrier, inc=1, device_id=exchange_peer(j), device_id_type=MESH)

    own_vel = pltpu.make_async_copy(va, vel.at[0], loc_sem.at[0])
    own_vel.start()
    own_modes = pltpu.make_async_copy(modes_in, modes, loc_sem.at[1])
    own_modes.start()
    own_small = pltpu.make_async_copy(small_in, small, loc_sem.at[2])
    own_small.start()
    pl.semaphore_wait(barrier, 16 + 4 * cross)

    def vel_copy(src, dst, k, to, half=None):
        s = va if src == 0 else vel.at[src] if half is None else vel.at[src, :, pl.ds(half, KD // 2)]
        d = vel.at[dst] if half is None else vel.at[dst, :, pl.ds(half, KD // 2)]
        return pltpu.make_async_remote_copy(
            src_ref=s, dst_ref=d, send_sem=vel_ss.at[k], recv_sem=vel_rs.at[k],
            device_id=to, device_id_type=MESH)

    c_x = vel_copy(0, 1, 0, dev(dx=1))
    c_yp = vel_copy(0, 6, 1, dev(dy=1))
    c_ym = vel_copy(0, 2, 2, dev(dy=3))
    c_xyp = vel_copy(1, 7, 3, dev(dy=1))
    c_xym = vel_copy(1, 3, 4, dev(dy=3))
    c_fyp = vel_copy(6, 4, 5, dev(dy=1), 0)
    c_fym = vel_copy(2, 4, 6, dev(dy=3), KD // 2)
    c_x2 = vel_copy(4, 5, 7, dev(dx=1), 0)
    c_x3 = vel_copy(4, 5, 8, dev(dx=1), KD // 2)
    c_yp.start()
    c_ym.start()
    c_x.start()
    own_small.wait()
    def zero_pad(n, _):
        grid_f[n // 4, 4 + n % 4, 96:104, :] = jnp.zeros((8, 128), F32)
        return 0

    lax.fori_loop(0, 20, zero_pad, 0)

    def mode_row(n, _):
        for h in range(2):
            f = small[FM + h * MH + n]
            msq[h, pl.ds(n, 1), :] = jnp.full((1, 128), f * f, F32)
            mdf[h, pl.ds(n, 1), :] = jnp.full((1, 128), 2.0 * small[FD + h * MH + n] * f, F32)
        return 0

    def mode_rows():
        lax.fori_loop(0, 96, mode_row, 0)
        for n in range(96, 104):
            f = small[FM + n]
            msq[0, n:n + 1, :] = jnp.full((1, 128), f * f, F32)
            mdf[0, n:n + 1, :] = jnp.full((1, 128), 2.0 * small[FD + n] * f, F32)
        msq[1, 96:104, :] = jnp.ones((8, 128), F32)
        mdf[1, 96:104, :] = jnp.ones((8, 128), F32)

    def prep(kt, _):
        lanes = pl.ds(pl.multiple_of(kt * 128, 128), 128)
        for c in range(3):
            vr = vb[c * 64:c * 64 + 32, lanes].astype(F32)
            vi = vb[c * 64 + 32:c * 64 + 64, lanes].astype(F32)
            vf[kt, c * 3] = vr
            vf[kt, c * 3 + 1] = vi - vr
            vf[kt, c * 3 + 2] = vr + vi
        return 0

    lax.fori_loop(0, KT, prep, 0)

    def sib_copy(j):
        return pltpu.make_async_remote_copy(
            src_ref=tx_sib.at[j], dst_ref=rx_sib.at[j], send_sem=sib_ss.at[j], recv_sem=sib_rs.at[j],
            device_id=dev(dc=1), device_id_type=MESH)

    def mine(dx):
        return cross == dx

    def send_sibling(j, dx):
        @pl.when(jnp.logical_not(mine(dx)))
        def _():
            def one(t, _):
                tx_sib[j, t] = grid_f[4, t].astype(BF16)
                return 0

            lax.fori_loop(0, 8, one, 0)
            sib_copy(j).start()

    def z_copy(d, n, j):
        hop = (1, 2, 1, 2)[n]
        return pltpu.make_async_remote_copy(
            src_ref=tx_z.at[d, n, j], dst_ref=rx_z.at[d, n, j],
            send_sem=z_ss.at[d, n, j], recv_sem=z_rs.at[d, n, j],
            device_id=dev(dz=hop if d == 0 else -hop), device_id_type=MESH)

    def a_copy(n, j):
        return pltpu.make_async_remote_copy(
            src_ref=tx_a.at[j], dst_ref=rx_a.at[n, j],
            send_sem=a_ss.at[n, j], recv_sem=a_rs.at[n, j],
            device_id=exchange_peer(j, n), device_id_type=MESH)

    def origin(j):
        dy, dx = group(j)
        return ((y + 4 - dy) % 4 // 2) * 2 + (xl + dx) % 2

    def g_copy(d, far, j):
        back = 0 if far <= 2 else 2
        src = (z - back + 8) % 8 if d == 0 else (z + back) % 8
        hop = far - back
        part = r_in.at[src, core, origin(j)]
        return pltpu.make_async_remote_copy(
            src_ref=part, dst_ref=part, send_sem=g_ss.at[d, far - 1, j], recv_sem=g_rs.at[d, far - 1, j],
            device_id=dev(dz=hop if d == 0 else -hop), device_id_type=MESH)

    def g_arrival(d, far, j):
        src = (z - far + 8) % 8 if d == 0 else (z + far) % 8
        part = r_in.at[src, core, origin(j)]
        return pltpu.make_async_remote_copy(
            src_ref=part, dst_ref=part, send_sem=g_ss.at[d, far - 1, j], recv_sem=g_rs.at[d, far - 1, j],
            device_id=dev(dc=1), device_id_type=MESH)

    def sib_chunk(dz, j, own=True):
        if own:
            where = origin(j)
        else:
            other = 1 - cross
            dy = (1 - other) * EVEN[j][0] + other * ODD[j][0]
            dx = (1 - other) * EVEN[j][1] + other * ODD[j][1]
            where = ((y + 4 - dy) % 4 // 2) * 2 + (xl + dx) % 2
        part = r_in.at[(z + dz + 8) % 8, core if own else 1 - core, where]
        return pltpu.make_async_remote_copy(
            src_ref=part, dst_ref=part, send_sem=gs_ss.at[dz + 4, j], recv_sem=gs_rs.at[dz + 4, j],
            device_id=dev(dc=1), device_id_type=MESH)

    lane = lax.broadcasted_iota(jnp.int32, (1, 128), 1)
    second = (lane // 32) % 2 == 1
    sign = jnp.where(lane < 64, -1.0, 1.0).astype(F32)

    def part_for(j, t):
        return grid_f[j, t] + rx_sib[j, t].astype(F32)

    def far_side(d, j):
        return j % 2 == d

    def z_first(j):
        sib_copy(j).wait_recv()
        for n, dist in ((0, 3), (1, 4), (2, 1)):
            for d in range(2):
                if n == 1 and not far_side(d, j):
                    continue
                t = (z + dist) % 8 if d == 0 else (z - dist + 8) % 8
                tx_z[d, n, j] = part_for(j, t).astype(BF16)
                z_copy(d, n, j).start()

    def z_second(j):
        for d in range(2):
            t = (z + 2) % 8 if d == 0 else (z - 2 + 8) % 8
            value = part_for(j, t)
            for n in range(2):
                if n == 0 or far_side(d, j):
                    z_copy(d, n, j).wait_recv()
                    value = value + rx_z[d, n, j].astype(F32)
            tx_z[d, 3, j] = value.astype(BF16)
            z_copy(d, 3, j).start()

    def exchange(j):
        value = part_for(j, z)
        for n in (2, 3):
            for d in range(2):
                z_copy(d, n, j).wait_recv()
                value = value + rx_z[d, n, j].astype(F32)
        value = value.astype(BF16)
        tx_a[j] = value
        a_copy(1, j).start()
        if j == 0:
            @pl.when(crossed)
            def _():
                a_copy(0, 0).start()

            @pl.when(jnp.logical_not(crossed))
            def _():
                rx_a[0, 0] = value
        else:
            a_copy(0, j).start()

    def respond(j):
        zh, zl = z // 4, z % 4
        gy, gx = group(j)
        other = ((y + 4 - gy) % 4) * 2 + (xl + gx) % 2
        w = jnp.where(second, small[zl * 2 + 1], small[zl * 2])
        for b in range(B32):
            w = jnp.where(lane % B32 == b, w + small[A8 + other * B32 + b], w)
        s2 = msq[zh]
        t = s2 - w * w
        g = mdf[zh] * w
        inv = 1.0 / (t * t + g * g)
        re = s2 * t * inv
        im = -s2 * g * inv * sign
        if j == 0:
            @pl.when(crossed)
            def _():
                a_copy(0, 0).wait_recv()
        else:
            a_copy(0, j).wait_recv()
        a_copy(1, j).wait_recv()
        f = rx_a[0, j].astype(F32) + rx_a[1, j].astype(F32)
        r_in[z, core, origin(j)] = (re * f + im * pltpu.roll(f, 64, 1)).astype(BF16)
        for far in (2, 1):
            for d in range(2):
                g_copy(d, far, j).start()
        sib_chunk(0, j).start()

    def g_second(j):
        for d in range(2):
            g_arrival(d, 2, j).wait_recv()
            g_copy(d, 3, j).start()
            if far_side(d, j):
                g_copy(d, 4, j).start()
        for d in range(2):
            sib_chunk(2 if d else -2, j).start()
        for d in range(2):
            g_arrival(d, 1, j).wait_recv()
            sib_chunk(1 if d else -1, j).start()

    def g_last(j):
        for d in range(2):
            g_arrival(d, 3, j).wait_recv()
            sib_chunk(3 if d else -3, j).start()
        g_arrival(j % 2, 4, j).wait_recv()
        sib_chunk(-4, j).start()

    def arrange(dz):
        for j in range(4):
            sib_chunk(dz, j, own=False).wait_recv()
        zc = (z + dz + 8) % 8
        zh, zl = zc // 4, zc % 4
        low, even = lane < 64, (lane // 32) % 2 == 0

        def half(hp, _):
            b = [r_in[zc, i // 2, hp * 2 + i % 2].astype(F32) for i in range(4)]
            u = [None] * 4
            for i in range(2):
                u[i] = jnp.where(low, b[i], pltpu.roll(b[i + 2], 64, 1))
                u[i + 2] = jnp.where(low, pltpu.roll(b[i], 64, 1), b[i + 2])
            w = [None] * 4
            for i in (0, 2):
                w[i] = jnp.where(even, u[i], pltpu.roll(u[i + 1], 32, 1))
                w[i + 1] = jnp.where(even, pltpu.roll(u[i], 96, 1), u[i + 1])
            for g in range(4):
                idx = (g // 2) * 8 + zl * 2 + g % 2
                rhs[idx, zh, :, pl.ds(pl.multiple_of(hp * 128, 128), 128)] = w[g].astype(BF16)
            return 0

        lax.fori_loop(0, 2, half, 0)

    STAGES = (z_first, z_second, exchange, respond, g_second, g_last)

    def stage(j, k):
        STAGES[k](j)
        if j == 3 and k == 4:
            arrange(0)
        if j == 3 and k == 5:
            for dz in (1, -1, 2, -2):
                arrange(dz)

    WHEN = ((3, 7, 8, 9, 10, 11),
            (5, 8, 9, 10, 11, 12),
            (7, 8, 9, 10, 11, 12),
            (8, 9, 10, 11, 12, 13))

    def events(t):
        return [(j, WHEN[j].index(t)) for j in (3, 2, 1, 0) if t in WHEN[j]]

    def forces(prs, h, dst):
        f = lax.dot_general(
            modes[...], prs[pl.ds(pl.multiple_of(h * 256, 256), 256), :], (((1,), (1,)), ((), ())),
            preferred_element_type=F32)
        for n in range(2):
            grid_f[dst, 2 * h + n] = f[0:104, n * 128:n * 128 + 128]
            grid_f[dst, 4 + 2 * h + n, 0:96] = f[104:200, n * 128:n * 128 + 128]

    def pressure(prs, slot, kt, k):
        lanes = pl.ds(pl.multiple_of(kt * 128, 128), 128)
        for c in range(3):
            both = vel[slot, c * 16:c * 16 + 16, lanes].astype(F32)
            ur, ui = both[0:8] * -0.5, both[8:16] * -0.5
            uf[k, c * 24:c * 24 + 8] = ur
            uf[k, c * 24 + 8:c * 24 + 16] = ui
            uf[k, c * 24 + 16:c * 24 + 24] = ur + ui
        for half in range(2):
            v = [vf[kt, n, half * 16:half * 16 + 16, :] for n in range(9)]
            for a in range(A8):
                row = (a // 2) * 128 + (a % 2) * 32 + half * 16
                k1 = k2 = k3 = None
                for c in range(3):
                    ur = uf[k, c * 24 + a:c * 24 + a + 1, :]
                    ui = uf[k, c * 24 + 8 + a:c * 24 + 8 + a + 1, :]
                    us = uf[k, c * 24 + 16 + a:c * 24 + 16 + a + 1, :]
                    t1, t2, t3 = v[c * 3] * us, v[c * 3 + 1] * ur, v[c * 3 + 2] * ui
                    k1 = t1 if k1 is None else k1 + t1
                    k2 = t2 if k2 is None else k2 + t2
                    k3 = t3 if k3 is None else k3 + t3
                prs[row:row + 16, lanes] = (k1 - k3).astype(BF16)
                prs[row + 64:row + 80, lanes] = (k1 + k2).astype(BF16)

    own_modes.wait()
    own_vel.wait()

    def double_block(j, _):
        slots = (j % 2 + 4 * (j // 2), 2 + 4 * (j % 2) + j // 2)
        for dx in range(2):
            slot = slots[dx]
            if dx == 0:
                @pl.when(j == 3)
                def _():
                    c_x2.wait_recv()
                    c_x3.wait_recv()
            else:
                @pl.when(j == 0)
                def _():
                    c_yp.wait_recv()
                    c_fyp.start()
                    c_ym.wait_recv()
                    c_fym.start()
                    c_x.wait_recv()
                    c_xym.start()
                    c_xyp.start()

                @pl.when(j == 1)
                def _():
                    c_fyp.wait_recv()
                    c_x2.start()
                    c_fym.wait_recv()
                    c_x3.start()

                @pl.when(j == 2)
                def _():
                    mode_rows()
                    c_xym.wait_recv()

                @pl.when(j == 3)
                def _():
                    c_xyp.wait_recv()

            for jj in range(4):
                for t in events(2 * jj + dx):
                    @pl.when(j == jj)
                    def _():
                        stage(*t)

            def half(h, _):
                for k in range(7):
                    pressure(prs, slot, h * 7 + k, k)
                return 0

            lax.fori_loop(0, 2, half, 0)
            dst = jnp.where(mine(dx), j, 4)

            def force_half(h, _):
                forces(prs, h, dst)
                return 0

            lax.fori_loop(0, 2, force_half, 0)
            send_sibling(j, dx)
        return 0

    lax.fori_loop(0, 4, double_block, 0)

    for t in range(8, 14):
        for j, k in events(t):
            stage(j, k)
    for dz in (3, -3, -4):
        arrange(dz)

    for cp in (c_x, c_yp, c_ym, c_xyp, c_xym, c_fyp, c_fym, c_x2, c_x3):
        cp.wait_send()

    def drain(j, _):
        sib_copy(j).wait_send()
        return 0

    lax.fori_loop(0, 4, drain, 0)
    for j in range(4):
        for n in range(4):
            for d in range(2):
                if n != 1 or far_side(d, j):
                    z_copy(d, n, j).wait_send()
    for j in range(1, 4):
        a_copy(0, j).wait_send()
    for j in range(4):
        a_copy(1, j).wait_send()

    @pl.when(crossed)
    def _():
        a_copy(0, 0).wait_send()

    for j in range(4):
        for far in range(1, 5):
            for d in range(2):
                if far < 4 or far_side(d, j):
                    g_copy(d, far, j).wait_send()
        for dz in range(-4, 4):
            sib_chunk(dz, j).wait_send()


def stress_kernel(ms, rhs, out, acc):
    count = out.shape[0]
    lhs = ms[...].T
    for ra in range(16):
        r = rhs[ra].reshape(2 * MH, 256)[:M]
        acc[ra] = lax.dot_general(
            lhs, r, (((1,), (0,)), ((), ())), preferred_element_type=F32).astype(BF16)
    to = lax.broadcasted_iota(jnp.int32, (128, 128), 0)
    of = lax.broadcasted_iota(jnp.int32, (128, 128), 1)
    swap = jnp.where((to % 8 == of // 16) & (to // 8 == of % 16), 1.0, 0.0).astype(BF16)
    for r_ in range(2):
        for e in range(0, count, 16):
            rows = jnp.concatenate([acc[r_ * 8 + a, e:e + 16, :] for a in range(A8)], 0)
            turned = lax.dot_general(swap, rows, (((1,), (0,)), ((), ())), preferred_element_type=F32)
            out[e:e + 16, r_] = turned.astype(BF16).reshape(16, A8, 256)


def local(vel_a, vel_b, panel_modes, modal_stress, freq_a, freq_b, mode_freq, damping):
    va = jnp.transpose(vel_a, (2, 1, 0, 3)).reshape(48, KD)
    vb = jnp.transpose(vel_b, (2, 1, 0, 3)).reshape(192, KD)
    small = jnp.concatenate([freq_a, freq_b, mode_freq, damping])
    vm = pl.BlockSpec(memory_space=pltpu.VMEM)
    hbm = pl.BlockSpec(memory_space=pltpu.HBM)
    dma = pltpu.SemaphoreType.DMA
    r = pl.pallas_call(
        main_kernel,
        out_shape=jax.ShapeDtypeStruct((16, 2, MH, 256), BF16),
        in_specs=[vm, vm, hbm, hbm],
        out_specs=vm,
        scratch_shapes=[
            pltpu.SMEM((A8 + 256 + 2 * M,), F32),
            pltpu.VMEM((M, KD), BF16),
            pltpu.VMEM((8, 2, 4, MH, 128), BF16),
            pltpu.VMEM((8, 48, KD), BF16),
            pltpu.VMEM((2, MH, 128), F32),
            pltpu.VMEM((2, MH, 128), F32),
            pltpu.VMEM((KT, 9, B32, 128), F32),
            pltpu.VMEM((7, 72, 128), F32),
            pltpu.VMEM((512, KD), BF16),
            pltpu.VMEM((5, 8, MH, 128), F32),
            pltpu.VMEM((4, 8, MH, 128), BF16),
            pltpu.VMEM((4, 8, MH, 128), BF16),
            pltpu.VMEM((2, 4, 4, MH, 128), BF16),
            pltpu.VMEM((2, 4, 4, MH, 128), BF16),
            pltpu.VMEM((4, MH, 128), BF16),
            pltpu.VMEM((2, 4, MH, 128), BF16),
            dma((9,)), dma((9,)), dma((4,)), dma((4,)),
            dma((2, 4, 4)), dma((2, 4, 4)),
            dma((2, 4)), dma((2, 4)), dma((2, 4, 4)), dma((2, 4, 4)), dma((8, 4)), dma((8, 4)),
            dma((3,)),
        ],
        compiler_params=pltpu.CompilerParams(
            collective_id=0, has_side_effects=True, vmem_limit_bytes=48 * 1024 * 1024),
    )(va, vb, panel_modes, small)
    elements = modal_stress.shape[1]
    tile = 256
    return pl.pallas_call(
        stress_kernel,
        out_shape=jax.ShapeDtypeStruct((elements, 2, A8, 256), BF16),
        grid=(elements // tile,),
        in_specs=[
            pl.BlockSpec((M, tile), lambda i: (0, i)),
            pl.BlockSpec((16, 2, MH, 256), lambda i: (0, 0, 0, 0)),
        ],
        out_specs=pl.BlockSpec((tile, 2, A8, 256), lambda i: (i, 0, 0, 0)),
        scratch_shapes=[pltpu.VMEM((16, tile, 256), BF16)],
        compiler_params=pltpu.CompilerParams(vmem_limit_bytes=48 * 1024 * 1024),
    )(modal_stress, r)


def solution(mesh):
    in_specs = (
        P("pair", None, None, "zone"),
        P("pair", None, None, "zone"),
        P(None, "zone"),
        P(None, "zone"),
        P("pair"),
        P(),
        P(),
        P(),
    )
    out_specs = P("zone", None, "pair", None)
    return jax.shard_map(local, mesh=mesh, in_specs=in_specs, out_specs=out_specs, check_vma=False)
```

```python
import functools

import jax
import jax.numpy as jnp
from jax import lax
from jax.experimental import pallas as pl
from jax.experimental.pallas import tpu as pltpu
from jax.sharding import PartitionSpec as P

MESH = pl.DeviceIdType.MESH
F32 = jnp.float32
BF16 = jnp.bfloat16

A8 = 8
B32 = 32
KD = 1792
KT = KD // 128
M = 200
FM, FD = 264, 464
MH = 104
EVEN = ((0, 0), (0, 1), (2, 0), (2, 1))
ODD = ((1, 0), (3, 0), (1, 1), (3, 1))


def main_kernel(
    va, vb, modes_in, small_in,
    rhs,
    small, modes, r_in, vel, msq, mdf, vf, uf, prs, grid_f,
    tx_sib, rx_sib, tx_z, rx_z, tx_a, rx_a,
    vel_ss, vel_rs, sib_ss, sib_rs, z_ss, z_rs,
    a_ss, a_rs, g_ss, g_rs, gs_ss, gs_rs, loc_sem,
):
    pair = lax.axis_index("pair")
    zone = lax.axis_index("zone")
    y, xl = pair // 2, pair % 2
    core, z, xh = zone % 2, (zone // 2) % 8, zone // 16

    def dev(dy=0, dx=0, dz=0, dh=0, dc=0):
        return (
            ((y + dy) % 4) * 2 + (xl + dx) % 2,
            (((xh + dh) % 2) * 8 + (z + dz + 8) % 8) * 2 + (core + dc) % 2,
        )

    cross = (y + core) % 2

    def group(j):
        dy = (1 - cross) * EVEN[j][0] + cross * ODD[j][0]
        dx = (1 - cross) * EVEN[j][1] + cross * ODD[j][1]
        return dy, dx

    def exchange_peer(j, dh=0):
        dy, dx = group(j)
        return (((y + dy) % 4) * 2 + (xl + dx) % 2, (((xh + dh) % 2) * 8 + z) * 2 + y % 2)

    crossed = cross == 1

    barrier = pltpu.get_barrier_semaphore()
    pair_peers = [(dy, dx) for dy in range(4) for dx in range(2) if (dy, dx) != (0, 0)]
    for dy, dx in pair_peers:
        pl.semaphore_signal(barrier, inc=1, device_id=dev(dy=dy, dx=dx), device_id_type=MESH)
    for kw in (dict(dc=1), dict(dz=1), dict(dz=-1), dict(dz=2), dict(dz=-2)):
        pl.semaphore_signal(barrier, inc=1, device_id=dev(**kw), device_id_type=MESH)

    for j in range(4):
        pl.semaphore_signal(barrier, inc=1, device_id=exchange_peer(j, 1), device_id_type=MESH)

    @pl.when(crossed)
    def _():
        for j in range(4):
            pl.semaphore_signal(barrier, inc=1, device_id=exchange_peer(j), device_id_type=MESH)

    own_vel = pltpu.make_async_copy(va, vel.at[0], loc_sem.at[0])
    own_vel.start()
    own_modes = pltpu.make_async_copy(modes_in, modes, loc_sem.at[1])
    own_modes.start()
    own_small = pltpu.make_async_copy(small_in, small, loc_sem.at[2])
    own_small.start()
    pl.semaphore_wait(barrier, 16 + 4 * cross)

    def vel_copy(src, dst, k, to, half=None):
        s = va if src == 0 else vel.at[src] if half is None else vel.at[src, :, pl.ds(half, KD // 2)]
        d = vel.at[dst] if half is None else vel.at[dst, :, pl.ds(half, KD // 2)]
        return pltpu.make_async_remote_copy(
            src_ref=s, dst_ref=d, send_sem=vel_ss.at[k], recv_sem=vel_rs.at[k],
            device_id=to, device_id_type=MESH)

    c_x = vel_copy(0, 1, 0, dev(dx=1))
    c_yp = vel_copy(0, 6, 1, dev(dy=1))
    c_ym = vel_copy(0, 2, 2, dev(dy=3))
    c_xyp = vel_copy(1, 7, 3, dev(dy=1))
    c_xym = vel_copy(1, 3, 4, dev(dy=3))
    c_fyp = vel_copy(6, 4, 5, dev(dy=1), 0)
    c_fym = vel_copy(2, 4, 6, dev(dy=3), KD // 2)
    c_x2 = vel_copy(4, 5, 7, dev(dx=1), 0)
    c_x3 = vel_copy(4, 5, 8, dev(dx=1), KD // 2)
    c_yp.start()
    c_ym.start()
    c_x.start()
    own_small.wait()
    def zero_pad(n, _):
        grid_f[n // 4, 4 + n % 4, 96:104, :] = jnp.zeros((8, 128), F32)
        return 0

    lax.fori_loop(0, 20, zero_pad, 0)

    def mode_row(n, _):
        for h in range(2):
            f = small[FM + h * MH + n]
            msq[h, pl.ds(n, 1), :] = jnp.full((1, 128), f * f, F32)
            mdf[h, pl.ds(n, 1), :] = jnp.full((1, 128), 2.0 * small[FD + h * MH + n] * f, F32)
        return 0

    def mode_rows():
        lax.fori_loop(0, 96, mode_row, 0)
        for n in range(96, 104):
            f = small[FM + n]
            msq[0, n:n + 1, :] = jnp.full((1, 128), f * f, F32)
            mdf[0, n:n + 1, :] = jnp.full((1, 128), 2.0 * small[FD + n] * f, F32)
        msq[1, 96:104, :] = jnp.ones((8, 128), F32)
        mdf[1, 96:104, :] = jnp.ones((8, 128), F32)

    def prep(kt, _):
        lanes = pl.ds(pl.multiple_of(kt * 128, 128), 128)
        for c in range(3):
            vr = vb[c * 64:c * 64 + 32, lanes].astype(F32)
            vi = vb[c * 64 + 32:c * 64 + 64, lanes].astype(F32)
            vf[kt, c * 3] = vr
            vf[kt, c * 3 + 1] = vi - vr
            vf[kt, c * 3 + 2] = vr + vi
        return 0

    lax.fori_loop(0, KT, prep, 0)

    def sib_copy(j):
        return pltpu.make_async_remote_copy(
            src_ref=tx_sib.at[j], dst_ref=rx_sib.at[j], send_sem=sib_ss.at[j], recv_sem=sib_rs.at[j],
            device_id=dev(dc=1), device_id_type=MESH)

    def mine(dx):
        return cross == dx

    def send_sibling(j, dx):
        @pl.when(jnp.logical_not(mine(dx)))
        def _():
            def one(t, _):
                tx_sib[j, t] = grid_f[4, t].astype(BF16)
                return 0

            lax.fori_loop(0, 8, one, 0)
            sib_copy(j).start()

    def z_copy(d, n, j):
        hop = (1, 2, 1, 2)[n]
        return pltpu.make_async_remote_copy(
            src_ref=tx_z.at[d, n, j], dst_ref=rx_z.at[d, n, j],
            send_sem=z_ss.at[d, n, j], recv_sem=z_rs.at[d, n, j],
            device_id=dev(dz=hop if d == 0 else -hop), device_id_type=MESH)

    def a_copy(n, j):
        return pltpu.make_async_remote_copy(
            src_ref=tx_a.at[j], dst_ref=rx_a.at[n, j],
            send_sem=a_ss.at[n, j], recv_sem=a_rs.at[n, j],
            device_id=exchange_peer(j, n), device_id_type=MESH)

    def origin(j):
        dy, dx = group(j)
        return ((y + 4 - dy) % 4 // 2) * 2 + (xl + dx) % 2

    def g_copy(d, far, j):
        back = 0 if far <= 2 else 2
        src = (z - back + 8) % 8 if d == 0 else (z + back) % 8
        hop = far - back
        part = r_in.at[src, core, origin(j)]
        return pltpu.make_async_remote_copy(
            src_ref=part, dst_ref=part, send_sem=g_ss.at[d, far - 1, j], recv_sem=g_rs.at[d, far - 1, j],
            device_id=dev(dz=hop if d == 0 else -hop), device_id_type=MESH)

    def g_arrival(d, far, j):
        src = (z - far + 8) % 8 if d == 0 else (z + far) % 8
        part = r_in.at[src, core, origin(j)]
        return pltpu.make_async_remote_copy(
            src_ref=part, dst_ref=part, send_sem=g_ss.at[d, far - 1, j], recv_sem=g_rs.at[d, far - 1, j],
            device_id=dev(dc=1), device_id_type=MESH)

    def sib_chunk(dz, j, own=True):
        if own:
            where = origin(j)
        else:
            other = 1 - cross
            dy = (1 - other) * EVEN[j][0] + other * ODD[j][0]
            dx = (1 - other) * EVEN[j][1] + other * ODD[j][1]
            where = ((y + 4 - dy) % 4 // 2) * 2 + (xl + dx) % 2
        part = r_in.at[(z + dz + 8) % 8, core if own else 1 - core, where]
        return pltpu.make_async_remote_copy(
            src_ref=part, dst_ref=part, send_sem=gs_ss.at[dz + 4, j], recv_sem=gs_rs.at[dz + 4, j],
            device_id=dev(dc=1), device_id_type=MESH)

    lane = lax.broadcasted_iota(jnp.int32, (1, 128), 1)
    second = (lane // 32) % 2 == 1
    sign = jnp.where(lane < 64, -1.0, 1.0).astype(F32)

    def part_for(j, t):
        return grid_f[j, t] + rx_sib[j, t].astype(F32)

    def far_side(d, j):
        return j % 2 == d

    def z_first(j):
        sib_copy(j).wait_recv()
        for n, dist in ((0, 3), (1, 4), (2, 1)):
            for d in range(2):
                if n == 1 and not far_side(d, j):
                    continue
                t = (z + dist) % 8 if d == 0 else (z - dist + 8) % 8
                tx_z[d, n, j] = part_for(j, t).astype(BF16)
                z_copy(d, n, j).start()

    def z_second(j):
        for d in range(2):
            t = (z + 2) % 8 if d == 0 else (z - 2 + 8) % 8
            value = part_for(j, t)
            for n in range(2):
                if n == 0 or far_side(d, j):
                    z_copy(d, n, j).wait_recv()
                    value = value + rx_z[d, n, j].astype(F32)
            tx_z[d, 3, j] = value.astype(BF16)
            z_copy(d, 3, j).start()

    def exchange(j):
        value = part_for(j, z)
        for n in (2, 3):
            for d in range(2):
                z_copy(d, n, j).wait_recv()
                value = value + rx_z[d, n, j].astype(F32)
        value = value.astype(BF16)
        tx_a[j] = value
        a_copy(1, j).start()
        if j == 0:
            @pl.when(crossed)
            def _():
                a_copy(0, 0).start()

            @pl.when(jnp.logical_not(crossed))
            def _():
                rx_a[0, 0] = value
        else:
            a_copy(0, j).start()

    def respond(j):
        zh, zl = z // 4, z % 4
        gy, gx = group(j)
        other = ((y + 4 - gy) % 4) * 2 + (xl + gx) % 2
        w = jnp.where(second, small[zl * 2 + 1], small[zl * 2])
        for b in range(B32):
            w = jnp.where(lane % B32 == b, w + small[A8 + other * B32 + b], w)
        s2 = msq[zh]
        t = s2 - w * w
        g = mdf[zh] * w
        inv = 1.0 / (t * t + g * g)
        re = s2 * t * inv
        im = -s2 * g * inv * sign
        if j == 0:
            @pl.when(crossed)
            def _():
                a_copy(0, 0).wait_recv()
        else:
            a_copy(0, j).wait_recv()
        a_copy(1, j).wait_recv()
        f = rx_a[0, j].astype(F32) + rx_a[1, j].astype(F32)
        r_in[z, core, origin(j)] = (re * f + im * pltpu.roll(f, 64, 1)).astype(BF16)
        for far in (2, 1):
            for d in range(2):
                g_copy(d, far, j).start()
        sib_chunk(0, j).start()

    def g_second(j):
        for d in range(2):
            g_arrival(d, 2, j).wait_recv()
            g_copy(d, 3, j).start()
            if far_side(d, j):
                g_copy(d, 4, j).start()
        for d in range(2):
            sib_chunk(2 if d else -2, j).start()
        for d in range(2):
            g_arrival(d, 1, j).wait_recv()
            sib_chunk(1 if d else -1, j).start()

    def g_last(j):
        for d in range(2):
            g_arrival(d, 3, j).wait_recv()
            sib_chunk(3 if d else -3, j).start()
        g_arrival(j % 2, 4, j).wait_recv()
        sib_chunk(-4, j).start()

    def arrange(dz):
        for j in range(4):
            sib_chunk(dz, j, own=False).wait_recv()
        zc = (z + dz + 8) % 8
        zh, zl = zc // 4, zc % 4
        low, even = lane < 64, (lane // 32) % 2 == 0

        def half(hp, _):
            b = [r_in[zc, i // 2, hp * 2 + i % 2].astype(F32) for i in range(4)]
            u = [None] * 4
            for i in range(2):
                u[i] = jnp.where(low, b[i], pltpu.roll(b[i + 2], 64, 1))
                u[i + 2] = jnp.where(low, pltpu.roll(b[i], 64, 1), b[i + 2])
            w = [None] * 4
            for i in (0, 2):
                w[i] = jnp.where(even, u[i], pltpu.roll(u[i + 1], 32, 1))
                w[i + 1] = jnp.where(even, pltpu.roll(u[i], 96, 1), u[i + 1])
            for g in range(4):
                idx = (g // 2) * 8 + zl * 2 + g % 2
                rhs[idx, zh, :, pl.ds(pl.multiple_of(hp * 128, 128), 128)] = w[g].astype(BF16)
            return 0

        lax.fori_loop(0, 2, half, 0)

    STAGES = (z_first, z_second, exchange, respond, g_second, g_last)

    def stage(j, k):
        STAGES[k](j)
        if j == 3 and k == 4:
            arrange(0)
        if j == 3 and k == 5:
            for dz in (1, -1, 2, -2):
                arrange(dz)

    WHEN = ((3, 7, 8, 9, 10, 11),
            (5, 8, 9, 10, 11, 12),
            (7, 8, 9, 10, 11, 12),
            (8, 9, 10, 11, 12, 13))

    def events(t):
        order = (0, 1, 2, 3) if t == 8 else (3, 2, 1, 0)
        return [(j, WHEN[j].index(t)) for j in order if t in WHEN[j]]

    def forces(prs, h, dst):
        f = lax.dot_general(
            modes[...], prs[pl.ds(pl.multiple_of(h * 256, 256), 256), :], (((1,), (1,)), ((), ())),
            preferred_element_type=F32)
        for n in range(2):
            grid_f[dst, 2 * h + n] = f[0:104, n * 128:n * 128 + 128]
            grid_f[dst, 4 + 2 * h + n, 0:96] = f[104:200, n * 128:n * 128 + 128]

    def pressure(prs, slot, kt, k):
        lanes = pl.ds(pl.multiple_of(kt * 128, 128), 128)
        for c in range(3):
            both = vel[slot, c * 16:c * 16 + 16, lanes].astype(F32)
            ur, ui = both[0:8] * -0.5, both[8:16] * -0.5
            uf[k, c * 24:c * 24 + 8] = ur
            uf[k, c * 24 + 8:c * 24 + 16] = ui
            uf[k, c * 24 + 16:c * 24 + 24] = ur + ui
        for half in range(2):
            v = [vf[kt, n, half * 16:half * 16 + 16, :] for n in range(9)]
            for a in range(A8):
                row = (a // 2) * 128 + (a % 2) * 32 + half * 16
                k1 = k2 = k3 = None
                for c in range(3):
                    ur = uf[k, c * 24 + a:c * 24 + a + 1, :]
                    ui = uf[k, c * 24 + 8 + a:c * 24 + 8 + a + 1, :]
                    us = uf[k, c * 24 + 16 + a:c * 24 + 16 + a + 1, :]
                    t1, t2, t3 = v[c * 3] * us, v[c * 3 + 1] * ur, v[c * 3 + 2] * ui
                    k1 = t1 if k1 is None else k1 + t1
                    k2 = t2 if k2 is None else k2 + t2
                    k3 = t3 if k3 is None else k3 + t3
                prs[row:row + 16, lanes] = (k1 - k3).astype(BF16)
                prs[row + 64:row + 80, lanes] = (k1 + k2).astype(BF16)

    own_modes.wait()
    own_vel.wait()

    def double_block(j, _):
        slots = (j % 2 + 4 * (j // 2), 2 + 4 * (j % 2) + j // 2)
        for dx in range(2):
            slot = slots[dx]
            if dx == 0:
                @pl.when(j == 3)
                def _():
                    c_x2.wait_recv()
                    c_x3.wait_recv()
            else:
                @pl.when(j == 0)
                def _():
                    c_yp.wait_recv()
                    c_fyp.start()
                    c_ym.wait_recv()
                    c_fym.start()
                    c_x.wait_recv()
                    c_xym.start()
                    c_xyp.start()

                @pl.when(j == 1)
                def _():
                    c_fyp.wait_recv()
                    c_x2.start()
                    c_fym.wait_recv()
                    c_x3.start()

                @pl.when(j == 2)
                def _():
                    mode_rows()
                    c_xym.wait_recv()

                @pl.when(j == 3)
                def _():
                    c_xyp.wait_recv()

            for jj in range(4):
                for t in events(2 * jj + dx):
                    @pl.when(j == jj)
                    def _():
                        stage(*t)

            def half(h, _):
                for k in range(7):
                    pressure(prs, slot, h * 7 + k, k)
                return 0

            lax.fori_loop(0, 2, half, 0)
            dst = jnp.where(mine(dx), j, 4)

            def force_half(h, _):
                forces(prs, h, dst)
                return 0

            lax.fori_loop(0, 2, force_half, 0)
            send_sibling(j, dx)
        return 0

    lax.fori_loop(0, 4, double_block, 0)

    for t in range(8, 14):
        for j, k in events(t):
            stage(j, k)
    for dz in (3, -3, -4):
        arrange(dz)

    for cp in (c_x, c_yp, c_ym, c_xyp, c_xym, c_fyp, c_fym, c_x2, c_x3):
        cp.wait_send()

    def drain(j, _):
        sib_copy(j).wait_send()
        return 0

    lax.fori_loop(0, 4, drain, 0)
    for j in range(4):
        for n in range(4):
            for d in range(2):
                if n != 1 or far_side(d, j):
                    z_copy(d, n, j).wait_send()
    for j in range(1, 4):
        a_copy(0, j).wait_send()
    for j in range(4):
        a_copy(1, j).wait_send()

    @pl.when(crossed)
    def _():
        a_copy(0, 0).wait_send()

    for j in range(4):
        for far in range(1, 5):
            for d in range(2):
                if far < 4 or far_side(d, j):
                    g_copy(d, far, j).wait_send()
        for dz in range(-4, 4):
            sib_chunk(dz, j).wait_send()


def stress_kernel(ms, rhs, out, acc):
    count = out.shape[0]
    lhs = ms[...].T
    for ra in range(16):
        r = rhs[ra].reshape(2 * MH, 256)[:M]
        acc[ra] = lax.dot_general(
            lhs, r, (((1,), (0,)), ((), ())), preferred_element_type=F32).astype(BF16)
    to = lax.broadcasted_iota(jnp.int32, (128, 128), 0)
    of = lax.broadcasted_iota(jnp.int32, (128, 128), 1)
    swap = jnp.where((to % 8 == of // 16) & (to // 8 == of % 16), 1.0, 0.0).astype(BF16)
    for r_ in range(2):
        for e in range(0, count, 16):
            rows = jnp.concatenate([acc[r_ * 8 + a, e:e + 16, :] for a in range(A8)], 0)
            turned = lax.dot_general(swap, rows, (((1,), (0,)), ((), ())), preferred_element_type=F32)
            out[e:e + 16, r_] = turned.astype(BF16).reshape(16, A8, 256)


def local(vel_a, vel_b, panel_modes, modal_stress, freq_a, freq_b, mode_freq, damping):
    va = jnp.transpose(vel_a, (2, 1, 0, 3)).reshape(48, KD)
    vb = jnp.transpose(vel_b, (2, 1, 0, 3)).reshape(192, KD)
    small = jnp.concatenate([freq_a, freq_b, mode_freq, damping])
    vm = pl.BlockSpec(memory_space=pltpu.VMEM)
    hbm = pl.BlockSpec(memory_space=pltpu.HBM)
    dma = pltpu.SemaphoreType.DMA
    r = pl.pallas_call(
        main_kernel,
        out_shape=jax.ShapeDtypeStruct((16, 2, MH, 256), BF16),
        in_specs=[vm, vm, hbm, hbm],
        out_specs=vm,
        scratch_shapes=[
            pltpu.SMEM((A8 + 256 + 2 * M,), F32),
            pltpu.VMEM((M, KD), BF16),
            pltpu.VMEM((8, 2, 4, MH, 128), BF16),
            pltpu.VMEM((8, 48, KD), BF16),
            pltpu.VMEM((2, MH, 128), F32),
            pltpu.VMEM((2, MH, 128), F32),
            pltpu.VMEM((KT, 9, B32, 128), F32),
            pltpu.VMEM((7, 72, 128), F32),
            pltpu.VMEM((512, KD), BF16),
            pltpu.VMEM((5, 8, MH, 128), F32),
            pltpu.VMEM((4, 8, MH, 128), BF16),
            pltpu.VMEM((4, 8, MH, 128), BF16),
            pltpu.VMEM((2, 4, 4, MH, 128), BF16),
            pltpu.VMEM((2, 4, 4, MH, 128), BF16),
            pltpu.VMEM((4, MH, 128), BF16),
            pltpu.VMEM((2, 4, MH, 128), BF16),
            dma((9,)), dma((9,)), dma((4,)), dma((4,)),
            dma((2, 4, 4)), dma((2, 4, 4)),
            dma((2, 4)), dma((2, 4)), dma((2, 4, 4)), dma((2, 4, 4)), dma((8, 4)), dma((8, 4)),
            dma((3,)),
        ],
        compiler_params=pltpu.CompilerParams(
            collective_id=0, has_side_effects=True, vmem_limit_bytes=48 * 1024 * 1024),
    )(va, vb, panel_modes, small)
    elements = modal_stress.shape[1]
    tile = 256
    return pl.pallas_call(
        stress_kernel,
        out_shape=jax.ShapeDtypeStruct((elements, 2, A8, 256), BF16),
        grid=(elements // tile,),
        in_specs=[
            pl.BlockSpec((M, tile), lambda i: (0, i)),
            pl.BlockSpec((16, 2, MH, 256), lambda i: (0, 0, 0, 0)),
        ],
        out_specs=pl.BlockSpec((tile, 2, A8, 256), lambda i: (i, 0, 0, 0)),
        scratch_shapes=[pltpu.VMEM((16, tile, 256), BF16)],
        compiler_params=pltpu.CompilerParams(vmem_limit_bytes=48 * 1024 * 1024),
    )(modal_stress, r)


def solution(mesh):
    in_specs = (
        P("pair", None, None, "zone"),
        P("pair", None, None, "zone"),
        P(None, "zone"),
        P(None, "zone"),
        P("pair"),
        P(),
        P(),
        P(),
    )
    out_specs = P("zone", None, "pair", None)
    return jax.shard_map(local, mesh=mesh, in_specs=in_specs, out_specs=out_specs, check_vma=False)
```
